32 devices in a mesh: wide: 8 (over z, y), narrow: 4 (over x, core).
Axes of the slice: x: 2, y: 2, z: 4, core: 2. Of those that a mesh axis runs over, the one named last changes fastest.
Arguments:
- images: bfloat16 [8192, 1152], P(('wide', 'narrow')), may hold values from -0.1875 to 0.1875
- texts: bfloat16 [8192, 1152], P(('wide', 'narrow')), may hold values from -0.1875 to 0.1875
- labels: int32 [8192], P(('wide', 'narrow')), may hold values from 0 to 8191, as said below
- log_scale: float32 [1], replicated, may hold values from 1 to 2.3
- bias: float32 [1], replicated, may hold values from -4 to -2
Outputs:
- grad_images: float32 [8192, 1152], P(('wide', 'narrow'))
- grad_texts: float32 [8192, 1152], P(('wide', 'narrow'))
The draws below stay inside these ranges and needn't reach their ends.
Inputs may be any that keep to these rules, and one draw needn't show every extreme that they name: labels_i names a text row of the same block of 256 rows as row i, and the labels of each block are a permutation of that block's rows.
All inputs are finite; a program needn't handle non-finite values.
Results may differ from the reference program's by a relative error of at most 0.0042.
Values may be sent and summed in bfloat16 or wider, within the bound.
A program may use at most 64 MiB of HBM per device.

```python
import jax
import jax.numpy as jnp
from jax import lax

D = 1152
BLOCK = 256
WINDOW = 4
BATCH = 8192
N_WIDE = 8
N_NARROW = 4


def draw_labels(key, part):
    key = jax.random.fold_in(key, 7)
    blocks = BATCH // BLOCK
    subkeys = jax.random.split(key, blocks)
    orders = jax.vmap(lambda single: jax.random.permutation(single, BLOCK))(subkeys)
    starts = jnp.arange(blocks, dtype=jnp.int32)[:, None] * BLOCK
    return (orders.astype(jnp.int32) + starts).reshape(BATCH)


def level_of(stream_key, shape, cuts, smallest, top_value):
    def one(dim, blocks):
        heights = jax.random.uniform(jax.random.fold_in(jax.random.fold_in(stream_key, 6), dim), (blocks,), jnp.float32, smallest / len(cuts), top_value / len(cuts))
        return jnp.repeat(jnp.exp(heights), shape[dim] // blocks).reshape((-1,) + (1,) * (len(shape) - dim - 1))

    factor_of = one(*cuts[0])
    for cut in cuts[1:]:
        factor_of = factor_of * one(*cut)
    return factor_of


def noise(stream_key, extent, spread, bound, shards=(), held_as=jnp.bfloat16):
    result = jax.random.normal(stream_key, extent, jnp.float32) * spread
    if len(shards) > 0:
        result = level_of(stream_key, extent, shards, -0.22, 0.18) * result
    return jnp.clip(result, min=-bound, max=bound).astype(held_as)


def setup_inputs(seed: int = 0) -> dict:
    keys = jax.random.split(jax.random.key(seed), 6)
    images = noise(keys[0], (BATCH, D), D ** -0.5, 0.1875, ((0, 32),))
    texts = noise(keys[1], (BATCH, D), D ** -0.5, 0.1875, ((0, 32),))
    labels = draw_labels(jax.random.fold_in(keys[5], 71), 0)
    log_scale = jnp.clip(jax.random.uniform(keys[3], (1,), jnp.float32, 1.0, 2.3), 1.0, 2.3)
    bias = jnp.clip(jax.random.uniform(keys[4], (1,), jnp.float32, -4.0, -2.0), -4.0, -2.0)
    return {"images": images, "texts": texts, "labels": labels, "log_scale": log_scale, "bias": bias}


EPS = 1e-06

def normalize(vectors):
    floats = vectors.astype(jnp.float32)
    inverse = lax.rsqrt(lax.optimization_barrier(jnp.sum(floats * floats, axis=-1, keepdims=True)) + EPS)
    return (floats * inverse, inverse)

def unit_backward(unit_rows, inverse, upstream):
    return inverse * (upstream - unit_rows * lax.optimization_barrier(jnp.sum(unit_rows * upstream, axis=-1, keepdims=True)))

def reference(images, texts, labels, log_scale, bias):
    grid_shape = (N_WIDE, N_NARROW, BLOCK, D)
    image_unit, image_inverse = normalize(images)
    text_unit, text_inverse = normalize(texts)
    image_half = lax.optimization_barrier(image_unit.astype(jnp.bfloat16)).astype(jnp.float32).reshape(grid_shape)
    text_half = lax.optimization_barrier(text_unit.astype(jnp.bfloat16)).astype(jnp.float32).reshape(grid_shape)
    temper = jnp.exp(log_scale[0])
    offset = bias[0]
    label_grid = labels.reshape(N_WIDE, N_NARROW, BLOCK, 1)
    index_grid = jnp.arange(BATCH, dtype=jnp.int32).reshape(N_WIDE, N_NARROW, 1, BLOCK)
    image_grad = jnp.zeros(grid_shape, jnp.float32)
    text_grad = jnp.zeros(grid_shape, jnp.float32)
    for wide_step in range(2):
        for narrow_step in range(WINDOW):
            offsets = (wide_step, narrow_step + wide_step * (WINDOW - 1))
            visitor = jnp.roll(text_half, offsets, axis=(0, 1))
            target = jnp.roll(index_grid, offsets, axis=(0, 1))
            scores = jnp.einsum('wnid,wnjd->wnij', image_half, visitor)
            logits = temper * scores + offset
            positive = (label_grid == target).astype(jnp.float32)
            residual = jax.nn.sigmoid(logits) - positive
            weighted = lax.optimization_barrier((temper * residual).astype(jnp.bfloat16)).astype(jnp.float32)
            image_grad = image_grad + jnp.einsum('wnij,wnjd->wnid', weighted, visitor)
            text_part = jnp.einsum('wnij,wnid->wnjd', weighted, image_half)
            text_grad = text_grad + jnp.roll(text_part, (-offsets[0], -offsets[1]), axis=(0, 1))
    grad_images = unit_backward(image_unit, image_inverse, image_grad.reshape(BATCH, D))
    grad_texts = unit_backward(text_unit, text_inverse, text_grad.reshape(BATCH, D))
    return (grad_images, grad_texts)
```

```python
import functools

import jax
import jax.numpy as jnp
from jax import lax
from jax.experimental import pallas as pl
from jax.experimental.pallas import tpu as pltpu
from jax.sharding import PartitionSpec as P

WINDOW = 4
EPS = 1e-06
CHUNKS = 4
IMAGE, TEXT = 0, 1
MESH = pl.DeviceIdType.MESH


def normalize(vectors):
    floats = vectors.astype(jnp.float32)
    inverse = lax.rsqrt(jnp.sum(floats * floats, axis=-1, keepdims=True) + EPS)
    return (floats * inverse, inverse)


def unit_backward(unit_rows, inverse, upstream):
    return inverse * (upstream - unit_rows * jnp.sum(unit_rows * upstream, axis=-1, keepdims=True))


def kernel(
    wide_count,
    narrow_count,
    log_scale_ref,
    bias_ref,
    images_ref,
    texts_ref,
    labels_ref,
    grad_images_ref,
    grad_texts_ref,
    blocks,
    grads,
    send_sem,
    recv_sem,
):
    rows = blocks.shape[2]
    piece = rows // CHUNKS
    wide = lax.axis_index("wide")
    narrow = lax.axis_index("narrow")
    relay = narrow_count == WINDOW

    def device(wide_step, narrow_index):
        return (lax.rem(wide + wide_step + wide_count, wide_count), narrow_index)

    if relay:
        partner = device(0, narrow + 1 - 2 * lax.rem(narrow, 2))
        across = device(0, lax.rem(narrow + 2, narrow_count))
        onward = {IMAGE: device(-1, narrow), TEXT: device(1, narrow)}
        neighbours = [partner, across, onward[IMAGE], onward[TEXT]]
    else:
        direct = {}
        for side, sign in ((IMAGE, -1), (TEXT, 1)):
            for slot in range(1, 2 * WINDOW):
                wide_back = slot // WINDOW
                narrow_back = slot - wide_back * WINDOW + wide_back * (WINDOW - 1)
                index = lax.rem(narrow + sign * narrow_back + narrow_count, narrow_count)
                direct[side, slot] = device(sign * wide_back, index)
        neighbours = list(direct.values())

    barrier = pltpu.get_barrier_semaphore()
    for neighbour in neighbours:
        pl.semaphore_signal(barrier, inc=1, device_id=neighbour, device_id_type=MESH)

    temper = jnp.exp(jnp.full((1, rows), log_scale_ref[0], jnp.float32))
    offset = bias_ref[0]
    sources = {IMAGE: images_ref, TEXT: texts_ref}
    started = []

    def part(chunk):
        return pl.ds(chunk * piece, piece)

    def message(side, source_slot, slot, chunk, target):
        return pltpu.make_async_remote_copy(
            src_ref=blocks.at[side, source_slot, part(chunk)],
            dst_ref=blocks.at[side, slot, part(chunk)],
            send_sem=send_sem.at[side, slot, chunk],
            recv_sem=recv_sem.at[side, slot, chunk],
            device_id=target,
            device_id_type=MESH,
        )

    def send(side, source_slot, slot, chunk, target):
        copy = message(side, source_slot, slot, chunk, target)
        copy.start()
        started.append(copy)

    def arrived(side, slot, chunk):
        message(side, slot, slot, chunk, neighbours[0]).wait_recv()

    for chunk in range(CHUNKS):
        for side in (IMAGE, TEXT):
            unit, _ = normalize(sources[side][part(chunk), :])
            blocks[side, 0, part(chunk), :] = unit.astype(jnp.bfloat16)
        if chunk == 0:
            pl.semaphore_wait(barrier, len(neighbours))
        for side in (IMAGE, TEXT):
            if relay:
                send(side, 0, 2, chunk, across)
                send(side, 0, 4, chunk, onward[side])
                send(side, 0, 1, chunk, partner)
            else:
                for slot in range(1, 2 * WINDOW):
                    send(side, 0, slot, chunk, direct[side, slot])

    def residual(own, visitor):
        scores = lax.dot_general(
            own, visitor, (((1,), (1,)), ((), ())), preferred_element_type=jnp.float32
        )
        return jax.nn.sigmoid(temper * scores + offset)

    base = (wide * narrow_count + narrow) * rows
    target = base + lax.broadcasted_iota(jnp.int32, (rows, rows), 0)
    positive = (labels_ref[...] == target).astype(jnp.float32)
    weighted = (temper * (residual(blocks[TEXT, 0], blocks[IMAGE, 0]) - positive)).astype(jnp.bfloat16)
    grads[TEXT] = jnp.dot(weighted, blocks[IMAGE, 0], preferred_element_type=jnp.float32)
    grads[IMAGE] = lax.dot_general(
        weighted, blocks[TEXT, 0], (((0,), (0,)), ((), ())), preferred_element_type=jnp.float32
    )

    def visit(first, last):
        count = last - first

        @pl.loop(0, 2 * count)
        def _(step):
            side = lax.rem(step, 2)
            slot = first + step // 2
            own = 1 - side
            visitor = blocks[side, slot]
            weighted = (temper * residual(blocks[own, 0], visitor)).astype(jnp.bfloat16)
            grads[own] += jnp.dot(weighted, visitor, preferred_element_type=jnp.float32)

    if relay:
        for chunk in range(CHUNKS):
            for side in (IMAGE, TEXT):
                arrived(side, 1, chunk)
        visit(1, 2)
        for chunk in range(CHUNKS):
            arrived(IMAGE, 2, chunk)
            send(IMAGE, 2, 6, chunk, onward[IMAGE])
            send(IMAGE, 2, 3, chunk, partner)
            arrived(TEXT, 4, chunk)
            send(TEXT, 4, 6, chunk, across)
            send(TEXT, 4, 5, chunk, partner)
            arrived(TEXT, 2, chunk)
            send(TEXT, 2, 3, chunk, partner)
            arrived(IMAGE, 4, chunk)
            send(IMAGE, 4, 5, chunk, partner)
        for chunk in range(CHUNKS):
            for side in (IMAGE, TEXT):
                arrived(side, 3, chunk)
                arrived(side, 5, chunk)
        visit(2, 6)
        for chunk in range(CHUNKS):
            for side in (IMAGE, TEXT):
                arrived(side, 6, chunk)
                send(side, 6, 7, chunk, partner)
        visit(6, 7)
        for chunk in range(CHUNKS):
            for side in (IMAGE, TEXT):
                arrived(side, 7, chunk)
        visit(7, 8)
    else:
        for slot in range(1, 2 * WINDOW):
            for chunk in range(CHUNKS):
                for side in (IMAGE, TEXT):
                    arrived(side, slot, chunk)
        visit(1, 2 * WINDOW)

    outs = {IMAGE: grad_images_ref, TEXT: grad_texts_ref}
    for side in (IMAGE, TEXT):
        for chunk in range(CHUNKS):
            unit, inverse = normalize(sources[side][part(chunk), :])
            outs[side][part(chunk), :] = unit_backward(unit, inverse, grads[side, part(chunk), :])
    for copy in started:
        copy.wait_send()


def shards(images, texts, labels, log_scale, bias):
    rows, depth = images.shape
    wide_count = lax.axis_size("wide")
    narrow_count = lax.axis_size("narrow")
    vmem = pl.BlockSpec(memory_space=pltpu.VMEM)
    smem = pl.BlockSpec(memory_space=pltpu.SMEM)
    out = jax.ShapeDtypeStruct((rows, depth), jnp.float32)
    pairs = 2 * 2 * WINDOW * rows * rows
    return pl.pallas_call(
        functools.partial(kernel, wide_count, narrow_count),
        out_shape=(out, out),
        in_specs=[smem, smem, vmem, vmem, vmem],
        out_specs=(vmem, vmem),
        scratch_shapes=[
            pltpu.VMEM((2, 2 * WINDOW, rows, depth), jnp.bfloat16),
            pltpu.VMEM((2, rows, depth), jnp.float32),
            pltpu.SemaphoreType.DMA((2, 2 * WINDOW, CHUNKS)),
            pltpu.SemaphoreType.DMA((2, 2 * WINDOW, CHUNKS)),
        ],
        compiler_params=pltpu.CompilerParams(
            collective_id=0, has_side_effects=True, vmem_limit_bytes=40 * 1024 * 1024
        ),
        cost_estimate=pl.CostEstimate(
            flops=4 * pairs * depth, bytes_accessed=12 * rows * depth, transcendentals=pairs
        ),
        name="window_grads",
    )(log_scale, bias, images, texts, labels.reshape(1, rows))


def solution(mesh):
    return jax.shard_map(
        shards,
        mesh=mesh,
        in_specs=(
            P(("wide", "narrow"), None),
            P(("wide", "narrow"), None),
            P(("wide", "narrow")),
            P(),
            P(),
        ),
        out_specs=(P(("wide", "narrow"), None), P(("wide", "narrow"), None)),
        check_vma=False,
    )
```

```python
import functools

import jax
import jax.numpy as jnp
from jax import lax
from jax.experimental import pallas as pl
from jax.experimental.pallas import tpu as pltpu
from jax.sharding import PartitionSpec as P

WINDOW = 4
EPS = 1e-06
CHUNKS = 4
MESH = pl.DeviceIdType.MESH


def normalize(vectors):
    floats = vectors.astype(jnp.float32)
    inverse = lax.rsqrt(jnp.sum(floats * floats, axis=-1, keepdims=True) + EPS)
    return (floats * inverse, inverse)


def unit_backward(unit_rows, inverse, upstream):
    return inverse * (upstream - unit_rows * jnp.sum(unit_rows * upstream, axis=-1, keepdims=True))


def kernel(
    wide_count,
    narrow_count,
    log_scale_ref,
    bias_ref,
    images_ref,
    texts_ref,
    labels_ref,
    grad_images_ref,
    grad_texts_ref,
    raw,
    labels_row,
    blocks,
    grads,
    load_sem,
    send_sem,
    recv_sem,
):
    rows = blocks.shape[2]
    piece = rows // CHUNKS
    wide = lax.axis_index("wide")
    narrow = lax.axis_index("narrow")
    relay = narrow_count == WINDOW and wide_count % 2 == 0
    odd = lax.rem(wide, 2)
    text_side = odd if relay else 0
    image_side = 1 - text_side

    def device(wide_step, narrow_index):
        return (lax.rem(wide + wide_step + wide_count, wide_count), narrow_index)

    if relay:
        partner = device(0, narrow + 1 - 2 * lax.rem(narrow, 2))
        across = device(0, lax.rem(narrow + 2, narrow_count))
        near = device(1 - 2 * odd, narrow)
        far = device(2 * odd - 1, narrow)
        neighbours = [partner, across, near, far]
    else:
        direct = {}
        for side, sign in ((0, 1), (1, -1)):
            for slot in range(1, 2 * WINDOW):
                wide_back = slot // WINDOW
                narrow_back = slot - wide_back * WINDOW + wide_back * (WINDOW - 1)
                index = lax.rem(narrow + sign * narrow_back + 2 * narrow_count, narrow_count)
                direct[side, slot] = device(sign * wide_back, index)
        neighbours = list(direct.values())

    loads = [
        pltpu.make_async_copy(images_ref, raw.at[image_side], load_sem.at[0]),
        pltpu.make_async_copy(texts_ref, raw.at[text_side], load_sem.at[1]),
        pltpu.make_async_copy(labels_ref, labels_row, load_sem.at[2]),
    ]
    for load in loads:
        load.start()
    barrier = pltpu.get_barrier_semaphore()
    for neighbour in neighbours:
        pl.semaphore_signal(barrier, inc=1, device_id=neighbour, device_id_type=MESH)

    temper = jnp.exp(jnp.full((1, rows), log_scale_ref[0], jnp.float32))
    offset = bias_ref[0]
    started = []

    def part(chunk):
        return pl.ds(chunk * piece, piece)

    def message(side, source_slot, to_side, slot, chunk, target):
        return pltpu.make_async_remote_copy(
            src_ref=blocks.at[side, source_slot, part(chunk)],
            dst_ref=blocks.at[to_side, slot, part(chunk)],
            send_sem=send_sem.at[to_side, slot, chunk],
            recv_sem=recv_sem.at[to_side, slot, chunk],
            device_id=target,
            device_id_type=MESH,
        )

    def send(side, source_slot, to_side, slot, chunk, target):
        copy = message(side, source_slot, to_side, slot, chunk, target)
        copy.start()
        started.append(copy)

    def arrived(side, slot, chunk):
        message(side, slot, side, slot, chunk, neighbours[0]).wait_recv()

    def all_arrived(slot):
        for chunk in range(CHUNKS):
            for side in (0, 1):
                arrived(side, slot, chunk)

    for load in loads:
        load.wait()
    for side in (0, 1):
        for chunk in range(CHUNKS):
            unit, _ = normalize(raw[side, part(chunk), :])
            blocks[side, 0, part(chunk), :] = unit.astype(jnp.bfloat16)
            if side == 0 and chunk == 0:
                pl.semaphore_wait(barrier, len(neighbours))
            if relay:
                send(side, 0, side, 2, chunk, across)
                send(side, 0, 1 - side, 4, chunk, far if side else near)
                send(side, 0, side, 1, chunk, partner)
            else:
                for slot in range(1, 2 * WINDOW):
                    send(side, 0, side, slot, chunk, direct[side, slot])

    def probability(own, visitor):
        scores = lax.dot_general(
            own, visitor, (((1,), (1,)), ((), ())), preferred_element_type=jnp.float32
        )
        return jax.nn.sigmoid(temper[:, : scores.shape[1]] * scores + offset)

    base = (wide * narrow_count + narrow) * rows
    target = base + lax.broadcasted_iota(jnp.int32, (rows, rows), 0)
    positive = (labels_row[...] == target).astype(jnp.float32)
    residual = probability(blocks[text_side, 0], blocks[image_side, 0]) - positive
    weighted = (temper * residual).astype(jnp.bfloat16)
    grads[text_side] = jnp.dot(weighted, blocks[image_side, 0], preferred_element_type=jnp.float32)
    grads[image_side] = lax.dot_general(
        weighted, blocks[text_side, 0], (((0,), (0,)), ((), ())), preferred_element_type=jnp.float32
    )

    def visit(first, last, start=0, count=rows):
        @pl.loop(0, 2 * (last - first))
        def _(step):
            side = lax.rem(step, 2)
            own = 1 - side
            visitor = blocks[side, first + step // 2, pl.ds(start, count), :]
            weighted = (temper[:, :count] * probability(blocks[own, 0], visitor)).astype(jnp.bfloat16)
            grads[own] += jnp.dot(weighted, visitor, preferred_element_type=jnp.float32)

    if relay:
        all_arrived(1)
        visit(1, 2)
        for chunk in range(CHUNKS):
            arrived(0, 2, chunk)
            send(0, 2, 1, 6, chunk, near)
            send(0, 2, 0, 3, chunk, partner)
            arrived(0, 4, chunk)
            send(0, 4, 0, 6, chunk, across)
            send(0, 4, 0, 5, chunk, partner)
            arrived(1, 4, chunk)
            send(1, 4, 1, 5, chunk, partner)
        all_arrived(5)
        visit(4, 6)
        for chunk in range(CHUNKS):
            arrived(1, 2, chunk)
            send(1, 2, 1, 3, chunk, partner)
        all_arrived(3)
        visit(2, 4)
        half = CHUNKS // 2
        for first in (0, half):
            for chunk in range(first, first + half):
                for side in (0, 1):
                    arrived(side, 6, chunk)
                    send(side, 6, side, 7, chunk, partner)
            visit(6, 7, first * piece, half * piece)
            for chunk in range(first, first + half):
                for side in (0, 1):
                    arrived(side, 7, chunk)
            visit(7, 8, first * piece, half * piece)
    else:
        for slot in range(1, 2 * WINDOW):
            all_arrived(slot)
        visit(1, 2 * WINDOW)

    for out, side in ((grad_images_ref, image_side), (grad_texts_ref, text_side)):
        for chunk in range(CHUNKS):
            unit, inverse = normalize(raw[side, part(chunk), :])
            out[part(chunk), :] = unit_backward(unit, inverse, grads[side, part(chunk), :])
    for copy in started:
        copy.wait_send()


def shards(images, texts, labels, log_scale, bias):
    rows, depth = images.shape
    wide_count = lax.axis_size("wide")
    narrow_count = lax.axis_size("narrow")
    vmem = pl.BlockSpec(memory_space=pltpu.VMEM)
    anywhere = pl.BlockSpec(memory_space=pl.ANY)
    smem = pl.BlockSpec(memory_space=pltpu.SMEM)
    out = jax.ShapeDtypeStruct((rows, depth), jnp.float32)
    pairs = 2 * 2 * WINDOW * rows * rows
    return pl.pallas_call(
        functools.partial(kernel, wide_count, narrow_count),
        out_shape=(out, out),
        in_specs=[smem, smem, anywhere, anywhere, anywhere],
        out_specs=(vmem, vmem),
        scratch_shapes=[
            pltpu.VMEM((2, rows, depth), images.dtype),
            pltpu.VMEM((1, rows), jnp.int32),
            pltpu.VMEM((2, 2 * WINDOW, rows, depth), jnp.bfloat16),
            pltpu.VMEM((2, rows, depth), jnp.float32),
            pltpu.SemaphoreType.DMA((3,)),
            pltpu.SemaphoreType.DMA((2, 2 * WINDOW, CHUNKS)),
            pltpu.SemaphoreType.DMA((2, 2 * WINDOW, CHUNKS)),
        ],
        compiler_params=pltpu.CompilerParams(
            collective_id=0, has_side_effects=True, vmem_limit_bytes=40 * 1024 * 1024
        ),
        cost_estimate=pl.CostEstimate(
            flops=4 * pairs * depth, bytes_accessed=12 * rows * depth, transcendentals=pairs
        ),
        name="window_grads",
    )(log_scale, bias, images, texts, labels.reshape(1, rows))


def solution(mesh):
    return jax.shard_map(
        shards,
        mesh=mesh,
        in_specs=(
            P(("wide", "narrow"), None),
            P(("wide", "narrow"), None),
            P(("wide", "narrow")),
            P(),
            P(),
        ),
        out_specs=(P(("wide", "narrow"), None), P(("wide", "narrow"), None)),
        check_vma=False,
    )
```

```python
import functools

import jax
import jax.numpy as jnp
from jax import lax
from jax.experimental import pallas as pl
from jax.experimental.pallas import tpu as pltpu
from jax.sharding import PartitionSpec as P

WINDOW = 4
EPS = 1e-06
CHUNKS = 4
MESH = pl.DeviceIdType.MESH


def normalize(vectors):
    floats = vectors.astype(jnp.float32)
    inverse = lax.rsqrt(jnp.sum(floats * floats, axis=-1, keepdims=True) + EPS)
    return (floats * inverse, inverse)


def unit_backward(unit_rows, inverse, upstream):
    return inverse * (upstream - unit_rows * jnp.sum(unit_rows * upstream, axis=-1, keepdims=True))


def place(wide_count, wide_step, narrow_index):
    return (lax.rem(lax.axis_index("wide") + wide_step + wide_count, wide_count), narrow_index)


def greet(neighbours):
    barrier = pltpu.get_barrier_semaphore()
    for neighbour in neighbours:
        pl.semaphore_signal(barrier, inc=1, device_id=neighbour, device_id_type=MESH)
    return barrier


def probability(own, visitor, temper, offset):
    scores = lax.dot_general(
        own, visitor, (((1,), (1,)), ((), ())), preferred_element_type=jnp.float32
    )
    return jax.nn.sigmoid(temper * scores + offset)


def pull(own, visitor, temper, offset):
    weighted = (temper * probability(own, visitor, temper, offset)).astype(jnp.bfloat16)
    return jnp.dot(weighted, visitor, preferred_element_type=jnp.float32)


def own_pairs(image_rows, text_rows, labels_row, anchor, temper, offset):
    rows = image_rows.shape[0]
    target = anchor * rows + lax.broadcasted_iota(jnp.int32, (rows, rows), 0)
    positive = (labels_row == target).astype(jnp.float32)
    residual = probability(text_rows, image_rows, temper, offset) - positive
    weighted = (temper * residual).astype(jnp.bfloat16)
    image_grad = lax.dot_general(
        weighted, text_rows, (((0,), (0,)), ((), ())), preferred_element_type=jnp.float32
    )
    return image_grad, jnp.dot(weighted, image_rows, preferred_element_type=jnp.float32)


IMAGE, TEXT, IMAGE_ACROSS, TEXT_BACK = range(4)
I0, I1, I2, I3, T0, T1, T4, T5 = range(8)


def relay_kernel(
    wide_count,
    narrow_count,
    log_scale_ref,
    bias_ref,
    images_ref,
    texts_ref,
    labels_ref,
    grad_images_ref,
    grad_texts_ref,
    raw,
    labels_row,
    blocks,
    grads,
    outbox,
    inbox,
    load_sem,
    send_sem,
    recv_sem,
    grad_send_sem,
    grad_recv_sem,
):
    rows = blocks.shape[1]
    piece = rows // CHUNKS
    half = CHUNKS // 2
    narrow = lax.axis_index("narrow")
    partner = place(wide_count, 0, narrow + 1 - 2 * lax.rem(narrow, 2))
    across = place(wide_count, 0, lax.rem(narrow + 2, narrow_count))
    forth = place(wide_count, 1, narrow)
    back = place(wide_count, -1, narrow)
    neighbours = [partner, across, forth, back]

    def part(chunk):
        return pl.ds(chunk * piece, piece)

    sources = ((I0, raw.at[IMAGE], images_ref), (T0, raw.at[TEXT], texts_ref))
    loads = [
        [
            pltpu.make_async_copy(ref.at[part(chunk)], target.at[part(chunk)], load_sem.at[number, chunk])
            for number, (_, target, ref) in enumerate(sources)
        ]
        for chunk in range(CHUNKS)
    ]
    for pair in loads:
        for load in pair:
            load.start()
    label_load = pltpu.make_async_copy(labels_ref, labels_row, load_sem.at[2, 0])
    label_load.start()
    barrier = greet(neighbours)

    temper = jnp.exp(jnp.full((1, 1), log_scale_ref[0], jnp.float32))
    offset = bias_ref[0]
    started = []

    def message(source, slot, chunk, target):
        return pltpu.make_async_remote_copy(
            src_ref=blocks.at[source, part(chunk)],
            dst_ref=blocks.at[slot, part(chunk)],
            send_sem=send_sem.at[slot, chunk],
            recv_sem=recv_sem.at[slot, chunk],
            device_id=target,
            device_id_type=MESH,
        )

    def send(source, slot, chunk, target):
        copy = message(source, slot, chunk, target)
        copy.start()
        started.append(copy)

    def arrived(slot, first=0, last=CHUNKS):
        for chunk in range(first, last):
            message(slot, slot, chunk, partner).wait_recv()

    def return_message(side, chunk):
        return pltpu.make_async_remote_copy(
            src_ref=outbox.at[side, part(chunk)],
            dst_ref=inbox.at[side, part(chunk)],
            send_sem=grad_send_sem.at[side, chunk],
            recv_sem=grad_recv_sem.at[side, chunk],
            device_id=back if side else across,
            device_id_type=MESH,
        )

    for chunk in range(CHUNKS):
        for load in loads[chunk]:
            load.wait()
        for slot, source, _ in sources:
            unit, _ = normalize(source[part(chunk), :])
            blocks[slot, part(chunk), :] = unit.astype(jnp.bfloat16)
        if chunk == 0:
            pl.semaphore_wait(barrier, len(neighbours))
        send(I0, I2, chunk, across)
        send(T0, T4, chunk, forth)
        send(I0, I1, chunk, partner)
        send(T0, T1, chunk, partner)

    span = half * piece

    def add(target, own, own_half, first, visitor_half=None, count=2, fresh=False):
        own_rows = slice(None) if own_half is None else pl.ds(own_half * span, span)
        visitor_rows = slice(None) if visitor_half is None else pl.ds(visitor_half * span, span)
        visitor = blocks[first : first + count, visitor_rows, :]
        visitor = visitor.reshape(visitor.shape[0] * visitor.shape[1], visitor.shape[2])
        value = pull(blocks[own, own_rows, :], visitor, temper, offset)
        grads[target, own_rows, :] = value if fresh else grads[target, own_rows, :] + value

    def give(side, own_half):
        target = TEXT_BACK if side else IMAGE_ACROSS
        for chunk in range(own_half * half, (own_half + 1) * half):
            outbox[side, part(chunk), :] = grads[target, part(chunk), :].astype(outbox.dtype)
            copy = return_message(side, chunk)
            copy.start()
            started.append(copy)

    label_load.wait()
    anchor = lax.axis_index("wide") * narrow_count + narrow
    grads[IMAGE], grads[TEXT] = own_pairs(
        blocks[I0], blocks[T0], labels_row[...], anchor, temper, offset
    )
    arrived(I1)
    arrived(T1)
    add(IMAGE, I0, None, T1, count=1)
    add(TEXT, T0, None, I1, count=1)

    for turn in (0, 1):
        for chunk in range(turn * half, (turn + 1) * half):
            arrived(I2, chunk, chunk + 1)
            send(I2, I3, chunk, partner)
            arrived(T4, chunk, chunk + 1)
            send(T4, T5, chunk, partner)
        add(IMAGE_ACROSS, I2, turn, T0, fresh=True)
        add(TEXT_BACK, T4, turn, I0, fresh=True)
        arrived(T5, turn * half, (turn + 1) * half)
        add(IMAGE_ACROSS, I2, 0, T4, turn)
        if turn == 1:
            give(IMAGE, 0)
        arrived(I3, turn * half, (turn + 1) * half)
        add(TEXT_BACK, T4, 0, I2, turn)
        if turn == 1:
            give(TEXT, 0)
    add(IMAGE_ACROSS, I2, 1, T4)
    give(IMAGE, 1)
    add(TEXT_BACK, T4, 1, I2)
    give(TEXT, 1)
    add(IMAGE, I0, None, T4)
    add(TEXT, T0, None, I2)

    stores = []
    for chunk in range(CHUNKS):
        for side, out in ((IMAGE, grad_images_ref), (TEXT, grad_texts_ref)):
            return_message(side, chunk).wait_recv()
            unit, inverse = normalize(raw[side, part(chunk), :])
            total = grads[side, part(chunk), :] + inbox[side, part(chunk), :].astype(jnp.float32)
            grads[side, part(chunk), :] = unit_backward(unit, inverse, total)
            stores.append(
                pltpu.make_async_copy(grads.at[side, part(chunk)], out.at[part(chunk)], load_sem.at[side, chunk])
            )
            stores[-1].start()
    for copy in started:
        copy.wait_send()
    for store in stores:
        store.wait()


def direct_kernel(
    wide_count,
    narrow_count,
    log_scale_ref,
    bias_ref,
    images_ref,
    texts_ref,
    labels_ref,
    grad_images_ref,
    grad_texts_ref,
    labels_row,
    blocks,
    grads,
    load_sem,
    send_sem,
    recv_sem,
):
    rows = blocks.shape[2]
    wide = lax.axis_index("wide")
    narrow = lax.axis_index("narrow")
    slots = 2 * WINDOW
    targets = {}
    for side, sign in ((IMAGE, -1), (TEXT, 1)):
        for slot in range(1, slots):
            wide_back = slot // WINDOW
            narrow_back = slot - wide_back * WINDOW + wide_back * (WINDOW - 1)
            index = lax.rem(narrow + sign * narrow_back + 2 * narrow_count, narrow_count)
            targets[side, slot] = place(wide_count, sign * wide_back, index)
    load = pltpu.make_async_copy(labels_ref, labels_row, load_sem.at[0])
    load.start()
    barrier = greet(targets.values())

    temper = jnp.exp(jnp.full((1, 1), log_scale_ref[0], jnp.float32))
    offset = bias_ref[0]
    sources = {IMAGE: images_ref, TEXT: texts_ref}
    for side in (IMAGE, TEXT):
        blocks[side, 0] = normalize(sources[side][...])[0].astype(jnp.bfloat16)
    pl.semaphore_wait(barrier, len(targets))
    copies = {}
    for slot in range(1, slots):
        for side in (IMAGE, TEXT):
            copies[side, slot] = pltpu.make_async_remote_copy(
                src_ref=blocks.at[side, 0],
                dst_ref=blocks.at[side, slot],
                send_sem=send_sem.at[side, slot],
                recv_sem=recv_sem.at[side, slot],
                device_id=targets[side, slot],
                device_id_type=MESH,
            )
            copies[side, slot].start()
    load.wait()
    grads[IMAGE], grads[TEXT] = own_pairs(
        blocks[IMAGE, 0], blocks[TEXT, 0], labels_row[...], wide * narrow_count + narrow, temper, offset
    )
    for copy in copies.values():
        copy.wait_recv()

    @pl.loop(2, 2 * slots)
    def _(step):
        side = lax.rem(step, 2)
        grads[1 - side] += pull(blocks[1 - side, 0], blocks[side, step // 2], temper, offset)

    for side, out in ((IMAGE, grad_images_ref), (TEXT, grad_texts_ref)):
        unit, inverse = normalize(sources[side][...])
        out[...] = unit_backward(unit, inverse, grads[side])
    for copy in copies.values():
        copy.wait_send()


def shards(images, texts, labels, log_scale, bias):
    rows, depth = images.shape
    wide_count = lax.axis_size("wide")
    narrow_count = lax.axis_size("narrow")
    vmem = pl.BlockSpec(memory_space=pltpu.VMEM)
    smem = pl.BlockSpec(memory_space=pltpu.SMEM)
    hbm = pl.BlockSpec(memory_space=pltpu.HBM)
    row = pltpu.VMEM((1, rows), jnp.int32)
    dma = pltpu.SemaphoreType.DMA
    out = jax.ShapeDtypeStruct((rows, depth), jnp.float32)
    pairs = 2 * 2 * WINDOW * rows * rows
    if narrow_count == WINDOW:
        body, held = relay_kernel, hbm
        scratch = [
            pltpu.VMEM((2, rows, depth), images.dtype),
            row,
            pltpu.VMEM((2 * WINDOW, rows, depth), jnp.bfloat16),
            pltpu.VMEM((4, rows, depth), jnp.float32),
            pltpu.VMEM((2, rows, depth), jnp.bfloat16),
            pltpu.VMEM((2, rows, depth), jnp.bfloat16),
            dma((3, CHUNKS)),
            dma((2 * WINDOW, CHUNKS)),
            dma((2 * WINDOW, CHUNKS)),
            dma((2, CHUNKS)),
            dma((2, CHUNKS)),
        ]
    else:
        body, held = direct_kernel, vmem
        scratch = [
            row,
            pltpu.VMEM((2, 2 * WINDOW, rows, depth), jnp.bfloat16),
            pltpu.VMEM((2, rows, depth), jnp.float32),
            dma((1,)),
            dma((2, 2 * WINDOW)),
            dma((2, 2 * WINDOW)),
        ]
    return pl.pallas_call(
        functools.partial(body, wide_count, narrow_count),
        out_shape=(out, out),
        in_specs=[smem, smem, held, held, hbm],
        out_specs=(held, held),
        scratch_shapes=scratch,
        compiler_params=pltpu.CompilerParams(
            collective_id=0, has_side_effects=True, vmem_limit_bytes=60 * 1024 * 1024
        ),
        cost_estimate=pl.CostEstimate(
            flops=4 * pairs * depth, bytes_accessed=12 * rows * depth, transcendentals=pairs
        ),
        name="window_grads",
    )(log_scale, bias, images, texts, labels.reshape(1, rows))


def solution(mesh):
    return jax.shard_map(
        shards,
        mesh=mesh,
        in_specs=(
            P(("wide", "narrow"), None),
            P(("wide", "narrow"), None),
            P(("wide", "narrow")),
            P(),
            P(),
        ),
        out_specs=(P(("wide", "narrow"), None), P(("wide", "narrow"), None)),
        check_vma=False,
    )
```

```python
import functools

import jax
import jax.numpy as jnp
from jax import lax
from jax.experimental import pallas as pl
from jax.experimental.pallas import tpu as pltpu
from jax.sharding import PartitionSpec as P

WINDOW = 4
EPS = 1e-06
CHUNKS = 4
MESH = pl.DeviceIdType.MESH


def normalize(vectors):
    floats = vectors.astype(jnp.float32)
    inverse = lax.rsqrt(jnp.sum(floats * floats, axis=-1, keepdims=True) + EPS)
    return (floats * inverse, inverse)


def unit_backward(unit_rows, inverse, upstream):
    return inverse * (upstream - unit_rows * jnp.sum(unit_rows * upstream, axis=-1, keepdims=True))


def place(wide_count, wide_step, narrow_index):
    return (lax.rem(lax.axis_index("wide") + wide_step + wide_count, wide_count), narrow_index)


def greet(neighbours):
    barrier = pltpu.get_barrier_semaphore()
    for neighbour in neighbours:
        pl.semaphore_signal(barrier, inc=1, device_id=neighbour, device_id_type=MESH)
    return barrier


def probability(own, visitor, temper, offset):
    scores = lax.dot_general(
        own, visitor, (((1,), (1,)), ((), ())), preferred_element_type=jnp.float32
    )
    return jax.nn.sigmoid(temper * scores + offset)


def pull(own, visitor, temper, offset):
    weighted = (temper * probability(own, visitor, temper, offset)).astype(jnp.bfloat16)
    return jnp.dot(weighted, visitor, preferred_element_type=jnp.float32)


def own_pairs(image_rows, text_rows, labels_row, anchor, temper, offset):
    rows = image_rows.shape[0]
    target = anchor * rows + lax.broadcasted_iota(jnp.int32, (rows, rows), 0)
    positive = (labels_row == target).astype(jnp.float32)
    residual = probability(text_rows, image_rows, temper, offset) - positive
    weighted = (temper * residual).astype(jnp.bfloat16)
    image_grad = lax.dot_general(
        weighted, text_rows, (((0,), (0,)), ((), ())), preferred_element_type=jnp.float32
    )
    return image_grad, jnp.dot(weighted, image_rows, preferred_element_type=jnp.float32)


IMAGE, TEXT, IMAGE_ACROSS, TEXT_BACK = range(4)
I0, I1, I2, I3, T0, T1, T4, T5 = range(8)


def relay_kernel(
    wide_count,
    narrow_count,
    log_scale_ref,
    bias_ref,
    images_ref,
    texts_ref,
    labels_ref,
    grad_images_ref,
    grad_texts_ref,
    raw,
    labels_row,
    blocks,
    grads,
    outbox,
    inbox,
    load_sem,
    send_sem,
    recv_sem,
    grad_send_sem,
    grad_recv_sem,
):
    rows = blocks.shape[1]
    piece = rows // CHUNKS
    half = CHUNKS // 2
    narrow = lax.axis_index("narrow")
    partner = place(wide_count, 0, narrow + 1 - 2 * lax.rem(narrow, 2))
    across = place(wide_count, 0, lax.rem(narrow + 2, narrow_count))
    forth = place(wide_count, 1, narrow)
    back = place(wide_count, -1, narrow)
    neighbours = [partner, across, forth, back]

    def part(chunk):
        return pl.ds(chunk * piece, piece)

    sources = ((I0, raw.at[IMAGE], images_ref), (T0, raw.at[TEXT], texts_ref))
    loads = [
        [
            pltpu.make_async_copy(ref.at[part(chunk)], target.at[part(chunk)], load_sem.at[number, chunk])
            for number, (_, target, ref) in enumerate(sources)
        ]
        for chunk in range(CHUNKS)
    ]
    for pair in loads:
        for load in pair:
            load.start()
    label_load = pltpu.make_async_copy(labels_ref, labels_row, load_sem.at[2, 0])
    label_load.start()
    barrier = greet(neighbours)

    temper = jnp.exp(jnp.full((1, 1), log_scale_ref[0], jnp.float32))
    offset = bias_ref[0]
    started = []

    def message(source, slot, chunk, target):
        return pltpu.make_async_remote_copy(
            src_ref=blocks.at[source, part(chunk)],
            dst_ref=blocks.at[slot, part(chunk)],
            send_sem=send_sem.at[slot, chunk],
            recv_sem=recv_sem.at[slot, chunk],
            device_id=target,
            device_id_type=MESH,
        )

    def send(source, slot, chunk, target):
        copy = message(source, slot, chunk, target)
        copy.start()
        started.append(copy)

    def arrived(slot, first=0, last=CHUNKS):
        for chunk in range(first, last):
            message(slot, slot, chunk, partner).wait_recv()

    def return_message(side, chunk):
        return pltpu.make_async_remote_copy(
            src_ref=outbox.at[side, part(chunk)],
            dst_ref=inbox.at[side, part(chunk)],
            send_sem=grad_send_sem.at[side, chunk],
            recv_sem=grad_recv_sem.at[side, chunk],
            device_id=back if side else across,
            device_id_type=MESH,
        )

    for chunk in range(CHUNKS):
        for load in loads[chunk]:
            load.wait()
        for slot, source, _ in sources:
            unit, _ = normalize(source[part(chunk), :])
            blocks[slot, part(chunk), :] = unit.astype(jnp.bfloat16)
        if chunk == 0:
            pl.semaphore_wait(barrier, len(neighbours))
        send(I0, I2, chunk, across)
        send(T0, T4, chunk, forth)
        send(I0, I1, chunk, partner)
        send(T0, T1, chunk, partner)

    span = half * piece

    def add(target, own, own_half, first, visitor_half=None, count=2, fresh=False):
        own_rows = slice(None) if own_half is None else pl.ds(own_half * span, span)
        visitor_rows = slice(None) if visitor_half is None else pl.ds(visitor_half * span, span)
        visitor = blocks[first : first + count, visitor_rows, :]
        visitor = visitor.reshape(visitor.shape[0] * visitor.shape[1], visitor.shape[2])
        value = pull(blocks[own, own_rows, :], visitor, temper, offset)
        grads[target, own_rows, :] = value if fresh else grads[target, own_rows, :] + value

    def give(side, own_half):
        target = TEXT_BACK if side else IMAGE_ACROSS
        for chunk in range(own_half * half, (own_half + 1) * half):
            outbox[side, part(chunk), :] = grads[target, part(chunk), :].astype(outbox.dtype)
            copy = return_message(side, chunk)
            copy.start()
            started.append(copy)

    label_load.wait()
    anchor = lax.axis_index("wide") * narrow_count + narrow
    grads[IMAGE], grads[TEXT] = own_pairs(
        blocks[I0], blocks[T0], labels_row[...], anchor, temper, offset
    )
    arrived(I1)
    arrived(T1)
    add(IMAGE, I0, None, T1, count=1)
    add(TEXT, T0, None, I1, count=1)

    for turn in (0, 1):
        for chunk in range(turn * half, (turn + 1) * half):
            arrived(I2, chunk, chunk + 1)
            send(I2, I3, chunk, partner)
            arrived(T4, chunk, chunk + 1)
            send(T4, T5, chunk, partner)
        add(IMAGE_ACROSS, I2, turn, T0, fresh=True)
        add(TEXT_BACK, T4, turn, I0, fresh=True)
        arrived(T5, turn * half, (turn + 1) * half)
        add(IMAGE_ACROSS, I2, 0, T4, turn)
        if turn == 1:
            give(IMAGE, 0)
        arrived(I3, turn * half, (turn + 1) * half)
        add(TEXT_BACK, T4, 0, I2, turn)
        if turn == 1:
            give(TEXT, 0)
    add(IMAGE_ACROSS, I2, 1, T4)
    give(IMAGE, 1)
    add(TEXT_BACK, T4, 1, I2)
    give(TEXT, 1)
    add(IMAGE, I0, None, T4)
    add(TEXT, T0, None, I2)

    for chunk in range(CHUNKS):
        for side, out in ((IMAGE, grad_images_ref), (TEXT, grad_texts_ref)):
            return_message(side, chunk).wait_recv()
            unit, inverse = normalize(raw[side, part(chunk), :])
            total = grads[side, part(chunk), :] + inbox[side, part(chunk), :].astype(jnp.float32)
            out[part(chunk), :] = unit_backward(unit, inverse, total)
    for copy in started:
        copy.wait_send()


def store_kernel(images_from, texts_from, images_to, texts_to, store_sem):
    stores = [
        pltpu.make_async_copy(images_from, images_to, store_sem.at[0]),
        pltpu.make_async_copy(texts_from, texts_to, store_sem.at[1]),
    ]
    for store in stores:
        store.start()
    for store in stores:
        store.wait()


def direct_kernel(
    wide_count,
    narrow_count,
    log_scale_ref,
    bias_ref,
    images_ref,
    texts_ref,
    labels_ref,
    grad_images_ref,
    grad_texts_ref,
    labels_row,
    blocks,
    grads,
    load_sem,
    send_sem,
    recv_sem,
):
    rows = blocks.shape[2]
    wide = lax.axis_index("wide")
    narrow = lax.axis_index("narrow")
    slots = 2 * WINDOW
    targets = {}
    for side, sign in ((IMAGE, -1), (TEXT, 1)):
        for slot in range(1, slots):
            wide_back = slot // WINDOW
            narrow_back = slot - wide_back * WINDOW + wide_back * (WINDOW - 1)
            index = lax.rem(narrow + sign * narrow_back + 2 * narrow_count, narrow_count)
            targets[side, slot] = place(wide_count, sign * wide_back, index)
    load = pltpu.make_async_copy(labels_ref, labels_row, load_sem.at[0])
    load.start()
    barrier = greet(targets.values())

    temper = jnp.exp(jnp.full((1, 1), log_scale_ref[0], jnp.float32))
    offset = bias_ref[0]
    sources = {IMAGE: images_ref, TEXT: texts_ref}
    for side in (IMAGE, TEXT):
        blocks[side, 0] = normalize(sources[side][...])[0].astype(jnp.bfloat16)
    pl.semaphore_wait(barrier, len(targets))
    copies = {}
    for slot in range(1, slots):
        for side in (IMAGE, TEXT):
            copies[side, slot] = pltpu.make_async_remote_copy(
                src_ref=blocks.at[side, 0],
                dst_ref=blocks.at[side, slot],
                send_sem=send_sem.at[side, slot],
                recv_sem=recv_sem.at[side, slot],
                device_id=targets[side, slot],
                device_id_type=MESH,
            )
            copies[side, slot].start()
    load.wait()
    grads[IMAGE], grads[TEXT] = own_pairs(
        blocks[IMAGE, 0], blocks[TEXT, 0], labels_row[...], wide * narrow_count + narrow, temper, offset
    )
    for copy in copies.values():
        copy.wait_recv()

    @pl.loop(2, 2 * slots)
    def _(step):
        side = lax.rem(step, 2)
        grads[1 - side] += pull(blocks[1 - side, 0], blocks[side, step // 2], temper, offset)

    for side, out in ((IMAGE, grad_images_ref), (TEXT, grad_texts_ref)):
        unit, inverse = normalize(sources[side][...])
        out[...] = unit_backward(unit, inverse, grads[side])
    for copy in copies.values():
        copy.wait_send()


def shards(images, texts, labels, log_scale, bias):
    rows, depth = images.shape
    wide_count = lax.axis_size("wide")
    narrow_count = lax.axis_size("narrow")
    vmem = pl.BlockSpec(memory_space=pltpu.VMEM)
    smem = pl.BlockSpec(memory_space=pltpu.SMEM)
    hbm = pl.BlockSpec(memory_space=pltpu.HBM)
    row = pltpu.VMEM((1, rows), jnp.int32)
    dma = pltpu.SemaphoreType.DMA
    out = jax.ShapeDtypeStruct((rows, depth), jnp.float32)
    pairs = 2 * 2 * WINDOW * rows * rows
    if narrow_count == WINDOW:
        body, held = relay_kernel, hbm
        scratch = [
            pltpu.VMEM((2, rows, depth), images.dtype),
            row,
            pltpu.VMEM((2 * WINDOW, rows, depth), jnp.bfloat16),
            pltpu.VMEM((4, rows, depth), jnp.float32),
            pltpu.VMEM((2, rows, depth), jnp.bfloat16),
            pltpu.VMEM((2, rows, depth), jnp.bfloat16),
            dma((3, CHUNKS)),
            dma((2 * WINDOW, CHUNKS)),
            dma((2 * WINDOW, CHUNKS)),
            dma((2, CHUNKS)),
            dma((2, CHUNKS)),
        ]
    else:
        body, held = direct_kernel, vmem
        scratch = [
            row,
            pltpu.VMEM((2, 2 * WINDOW, rows, depth), jnp.bfloat16),
            pltpu.VMEM((2, rows, depth), jnp.float32),
            dma((1,)),
            dma((2, 2 * WINDOW)),
            dma((2, 2 * WINDOW)),
        ]
    arrays = (images, texts, labels.reshape(1, rows))
    if held is hbm:
        arrays = tuple(pltpu.with_memory_space_constraint(array, pltpu.HBM) for array in arrays)
    grads = pl.pallas_call(
        functools.partial(body, wide_count, narrow_count),
        out_shape=(out, out),
        in_specs=[smem, smem, held, held, hbm],
        out_specs=(vmem, vmem),
        scratch_shapes=scratch,
        compiler_params=pltpu.CompilerParams(
            collective_id=0, has_side_effects=True, vmem_limit_bytes=40 * 1024 * 1024
        ),
        cost_estimate=pl.CostEstimate(
            flops=4 * pairs * depth, bytes_accessed=12 * rows * depth, transcendentals=pairs
        ),
        name="window_grads",
    )(log_scale, bias, *arrays)
    anywhere = pl.BlockSpec(memory_space=pl.ANY)
    return pl.pallas_call(
        store_kernel,
        out_shape=(out, out),
        in_specs=[anywhere, anywhere],
        out_specs=(hbm, hbm),
        scratch_shapes=[dma((2,))],
        name="store",
    )(*grads)


def solution(mesh):
    return jax.shard_map(
        shards,
        mesh=mesh,
        in_specs=(
            P(("wide", "narrow"), None),
            P(("wide", "narrow"), None),
            P(("wide", "narrow")),
            P(),
            P(),
        ),
        out_specs=(P(("wide", "narrow"), None), P(("wide", "narrow"), None)),
        check_vma=False,
    )
```

```python
import functools

import jax
import jax.numpy as jnp
from jax import lax
from jax.experimental import pallas as pl
from jax.experimental.pallas import tpu as pltpu
from jax.sharding import PartitionSpec as P

WINDOW = 4
EPS = 1e-06
CHUNKS = 4
MESH = pl.DeviceIdType.MESH


def normalize(vectors):
    floats = vectors.astype(jnp.float32)
    inverse = lax.rsqrt(jnp.sum(floats * floats, axis=-1, keepdims=True) + EPS)
    return (floats * inverse, inverse)


def unit_backward(unit_rows, inverse, upstream):
    return inverse * (upstream - unit_rows * jnp.sum(unit_rows * upstream, axis=-1, keepdims=True))


def place(wide_count, wide_step, narrow_index):
    return (lax.rem(lax.axis_index("wide") + wide_step + wide_count, wide_count), narrow_index)


def greet(neighbours):
    barrier = pltpu.get_barrier_semaphore()
    for neighbour in neighbours:
        pl.semaphore_signal(barrier, inc=1, device_id=neighbour, device_id_type=MESH)
    return barrier


def probability(own, visitor, temper, offset):
    scores = lax.dot_general(
        own, visitor, (((1,), (1,)), ((), ())), preferred_element_type=jnp.float32
    )
    return jax.nn.sigmoid(temper * scores + offset)


def pull(own, visitor, temper, offset):
    weighted = (temper * probability(own, visitor, temper, offset)).astype(jnp.bfloat16)
    return jnp.dot(weighted, visitor, preferred_element_type=jnp.float32)


def own_pairs(image_rows, text_rows, labels_row, anchor, temper, offset):
    rows = image_rows.shape[0]
    target = anchor * rows + lax.broadcasted_iota(jnp.int32, (rows, rows), 0)
    positive = (labels_row == target).astype(jnp.float32)
    residual = probability(text_rows, image_rows, temper, offset) - positive
    weighted = (temper * residual).astype(jnp.bfloat16)
    image_grad = lax.dot_general(
        weighted, text_rows, (((0,), (0,)), ((), ())), preferred_element_type=jnp.float32
    )
    return image_grad, jnp.dot(weighted, image_rows, preferred_element_type=jnp.float32)


IMAGE, TEXT, IMAGE_ACROSS, TEXT_BACK = range(4)
I0, I1, I2, I3, T0, T1, T4, T5 = range(8)


def relay_kernel(
    wide_count,
    narrow_count,
    log_scale_ref,
    bias_ref,
    images_ref,
    texts_ref,
    labels_ref,
    grad_images_ref,
    grad_texts_ref,
    raw,
    labels_row,
    blocks,
    grads,
    outbox,
    inbox,
    load_sem,
    send_sem,
    recv_sem,
    grad_send_sem,
    grad_recv_sem,
):
    rows = blocks.shape[1]
    piece = rows // CHUNKS
    half = CHUNKS // 2
    narrow = lax.axis_index("narrow")
    partner = place(wide_count, 0, narrow + 1 - 2 * lax.rem(narrow, 2))
    across = place(wide_count, 0, lax.rem(narrow + 2, narrow_count))
    forth = place(wide_count, 1, narrow)
    back = place(wide_count, -1, narrow)
    neighbours = [partner, across, forth, back]

    def part(chunk):
        return pl.ds(chunk * piece, piece)

    sources = ((I0, raw.at[IMAGE], images_ref), (T0, raw.at[TEXT], texts_ref))
    loads = [
        [
            pltpu.make_async_copy(ref.at[part(chunk)], target.at[part(chunk)], load_sem.at[number, chunk])
            for number, (_, target, ref) in enumerate(sources)
        ]
        for chunk in range(CHUNKS)
    ]
    for pair in loads:
        for load in pair:
            load.start()
    label_load = pltpu.make_async_copy(labels_ref, labels_row, load_sem.at[2, 0])
    label_load.start()
    barrier = greet(neighbours)

    temper = jnp.exp(jnp.full((1, 1), log_scale_ref[0], jnp.float32))
    offset = bias_ref[0]
    started = []

    def message(source, slot, chunk, target):
        return pltpu.make_async_remote_copy(
            src_ref=blocks.at[source, part(chunk)],
            dst_ref=blocks.at[slot, part(chunk)],
            send_sem=send_sem.at[slot, chunk],
            recv_sem=recv_sem.at[slot, chunk],
            device_id=target,
            device_id_type=MESH,
        )

    def send(source, slot, chunk, target):
        copy = message(source, slot, chunk, target)
        copy.start()
        started.append(copy)

    def arrived(slot, first=0, last=CHUNKS):
        for chunk in range(first, last):
            message(slot, slot, chunk, partner).wait_recv()

    def return_message(side, chunk):
        return pltpu.make_async_remote_copy(
            src_ref=outbox.at[side, part(chunk)],
            dst_ref=inbox.at[side, part(chunk)],
            send_sem=grad_send_sem.at[side, chunk],
            recv_sem=grad_recv_sem.at[side, chunk],
            device_id=back if side else across,
            device_id_type=MESH,
        )

    for chunk in range(CHUNKS):
        for load in loads[chunk]:
            load.wait()
        for slot, source, _ in sources:
            unit, _ = normalize(source[part(chunk), :])
            blocks[slot, part(chunk), :] = unit.astype(jnp.bfloat16)
        if chunk == 0:
            pl.semaphore_wait(barrier, len(neighbours))
        send(I0, I2, chunk, across)
        send(T0, T4, chunk, forth)
        send(I0, I1, chunk, partner)
        send(T0, T1, chunk, partner)

    def cut(half_or_all):
        return slice(None) if half_or_all is None else pl.ds(half_or_all * half * piece, half * piece)

    def add(target, own, own_half, first, rows_of_each=slice(None), count=2, fresh=False):
        visitor = blocks[first : first + count, rows_of_each, :]
        visitor = visitor.reshape(visitor.shape[0] * visitor.shape[1], visitor.shape[2])
        value = pull(blocks[own, cut(own_half), :], visitor, temper, offset)
        grads[target, cut(own_half), :] = value if fresh else grads[target, cut(own_half), :] + value

    def pass_on(chunk):
        arrived(T4, chunk, chunk + 1)
        send(T4, T5, chunk, partner)
        arrived(I2, chunk, chunk + 1)
        send(I2, I3, chunk, partner)

    def give(side, own_half):
        target = TEXT_BACK if side else IMAGE_ACROSS
        for chunk in range(own_half * half, (own_half + 1) * half):
            outbox[side, part(chunk), :] = grads[target, part(chunk), :].astype(outbox.dtype)
            copy = return_message(side, chunk)
            copy.start()
            started.append(copy)

    label_load.wait()
    anchor = lax.axis_index("wide") * narrow_count + narrow
    grads[IMAGE], grads[TEXT] = own_pairs(
        blocks[I0], blocks[T0], labels_row[...], anchor, temper, offset
    )
    arrived(I1)
    arrived(T1)
    add(IMAGE, I0, None, T1, count=1)
    add(TEXT, T0, None, I1, count=1)

    for chunk in range(half):
        pass_on(chunk)
    add(IMAGE_ACROSS, I2, 0, T0, fresh=True)
    add(TEXT_BACK, T4, 0, I0, fresh=True)
    arrived(T5, 0, half)
    add(IMAGE_ACROSS, I2, 0, T4, cut(0))
    arrived(I3, 0, half)
    add(TEXT_BACK, T4, 0, I2, cut(0))
    for chunk in range(half, CHUNKS):
        pass_on(chunk)
        arrived(T5, chunk, chunk + 1)
        add(IMAGE_ACROSS, I2, 0, T4, part(chunk))
        if chunk == CHUNKS - 1:
            give(IMAGE, 0)
        arrived(I3, chunk, chunk + 1)
        add(TEXT_BACK, T4, 0, I2, part(chunk))
    give(TEXT, 0)
    add(IMAGE_ACROSS, I2, 1, T0, count=4, fresh=True)
    give(IMAGE, 1)
    add(TEXT_BACK, T4, 1, I0, count=4, fresh=True)
    give(TEXT, 1)
    add(IMAGE, I0, None, T4)
    add(TEXT, T0, None, I2)

    for chunk in range(CHUNKS):
        for side, out in ((IMAGE, grad_images_ref), (TEXT, grad_texts_ref)):
            return_message(side, chunk).wait_recv()
            unit, inverse = normalize(raw[side, part(chunk), :])
            total = grads[side, part(chunk), :] + inbox[side, part(chunk), :].astype(jnp.float32)
            out[part(chunk), :] = unit_backward(unit, inverse, total)
    for copy in started:
        copy.wait_send()


def direct_kernel(
    wide_count,
    narrow_count,
    log_scale_ref,
    bias_ref,
    images_ref,
    texts_ref,
    labels_ref,
    grad_images_ref,
    grad_texts_ref,
    labels_row,
    blocks,
    grads,
    load_sem,
    send_sem,
    recv_sem,
):
    rows = blocks.shape[2]
    wide = lax.axis_index("wide")
    narrow = lax.axis_index("narrow")
    slots = 2 * WINDOW
    targets = {}
    for side, sign in ((IMAGE, -1), (TEXT, 1)):
        for slot in range(1, slots):
            wide_back = slot // WINDOW
            narrow_back = slot - wide_back * WINDOW + wide_back * (WINDOW - 1)
            index = lax.rem(narrow + sign * narrow_back + 2 * narrow_count, narrow_count)
            targets[side, slot] = place(wide_count, sign * wide_back, index)
    load = pltpu.make_async_copy(labels_ref, labels_row, load_sem.at[0])
    load.start()
    barrier = greet(targets.values())

    temper = jnp.exp(jnp.full((1, 1), log_scale_ref[0], jnp.float32))
    offset = bias_ref[0]
    sources = {IMAGE: images_ref, TEXT: texts_ref}
    for side in (IMAGE, TEXT):
        blocks[side, 0] = normalize(sources[side][...])[0].astype(jnp.bfloat16)
    pl.semaphore_wait(barrier, len(targets))
    copies = {}
    for slot in range(1, slots):
        for side in (IMAGE, TEXT):
            copies[side, slot] = pltpu.make_async_remote_copy(
                src_ref=blocks.at[side, 0],
                dst_ref=blocks.at[side, slot],
                send_sem=send_sem.at[side, slot],
                recv_sem=recv_sem.at[side, slot],
                device_id=targets[side, slot],
                device_id_type=MESH,
            )
            copies[side, slot].start()
    load.wait()
    grads[IMAGE], grads[TEXT] = own_pairs(
        blocks[IMAGE, 0], blocks[TEXT, 0], labels_row[...], wide * narrow_count + narrow, temper, offset
    )
    for copy in copies.values():
        copy.wait_recv()

    @pl.loop(2, 2 * slots)
    def _(step):
        side = lax.rem(step, 2)
        grads[1 - side] += pull(blocks[1 - side, 0], blocks[side, step // 2], temper, offset)

    for side, out in ((IMAGE, grad_images_ref), (TEXT, grad_texts_ref)):
        unit, inverse = normalize(sources[side][...])
        out[...] = unit_backward(unit, inverse, grads[side])
    for copy in copies.values():
        copy.wait_send()


def shards(images, texts, labels, log_scale, bias):
    rows, depth = images.shape
    wide_count = lax.axis_size("wide")
    narrow_count = lax.axis_size("narrow")
    vmem = pl.BlockSpec(memory_space=pltpu.VMEM)
    smem = pl.BlockSpec(memory_space=pltpu.SMEM)
    hbm = pl.BlockSpec(memory_space=pltpu.HBM)
    row = pltpu.VMEM((1, rows), jnp.int32)
    dma = pltpu.SemaphoreType.DMA
    out = jax.ShapeDtypeStruct((rows, depth), jnp.float32)
    pairs = 2 * 2 * WINDOW * rows * rows
    if narrow_count == WINDOW:
        body, held = relay_kernel, hbm
        scratch = [
            pltpu.VMEM((2, rows, depth), images.dtype),
            row,
            pltpu.VMEM((2 * WINDOW, rows, depth), jnp.bfloat16),
            pltpu.VMEM((4, rows, depth), jnp.float32),
            pltpu.VMEM((2, rows, depth), jnp.bfloat16),
            pltpu.VMEM((2, rows, depth), jnp.bfloat16),
            dma((3, CHUNKS)),
            dma((2 * WINDOW, CHUNKS)),
            dma((2 * WINDOW, CHUNKS)),
            dma((2, CHUNKS)),
            dma((2, CHUNKS)),
        ]
    else:
        body, held = direct_kernel, vmem
        scratch = [
            row,
            pltpu.VMEM((2, 2 * WINDOW, rows, depth), jnp.bfloat16),
            pltpu.VMEM((2, rows, depth), jnp.float32),
            dma((1,)),
            dma((2, 2 * WINDOW)),
            dma((2, 2 * WINDOW)),
        ]
    arrays = (images, texts, labels.reshape(1, rows))
    if held is hbm:
        arrays = tuple(pltpu.with_memory_space_constraint(array, pltpu.HBM) for array in arrays)
    return pl.pallas_call(
        functools.partial(body, wide_count, narrow_count),
        out_shape=(out, out),
        in_specs=[smem, smem, held, held, hbm],
        out_specs=(vmem, vmem),
        scratch_shapes=scratch,
        compiler_params=pltpu.CompilerParams(
            collective_id=0, has_side_effects=True, vmem_limit_bytes=40 * 1024 * 1024
        ),
        cost_estimate=pl.CostEstimate(
            flops=4 * pairs * depth, bytes_accessed=12 * rows * depth, transcendentals=pairs
        ),
        name="window_grads",
    )(log_scale, bias, *arrays)

def solution(mesh):
    return jax.shard_map(
        shards,
        mesh=mesh,
        in_specs=(
            P(("wide", "narrow"), None),
            P(("wide", "narrow"), None),
            P(("wide", "narrow")),
            P(),
            P(),
        ),
        out_specs=(P(("wide", "narrow"), None), P(("wide", "narrow"), None)),
        check_vma=False,
    )
```

```python
import functools

import jax
import jax.numpy as jnp
from jax import lax
from jax.experimental import pallas as pl
from jax.experimental.pallas import tpu as pltpu
from jax.sharding import PartitionSpec as P

WINDOW = 4
EPS = 1e-06
CHUNKS = 8
MESH = pl.DeviceIdType.MESH


def normalize(vectors):
    floats = vectors.astype(jnp.float32)
    inverse = lax.rsqrt(jnp.sum(floats * floats, axis=-1, keepdims=True) + EPS)
    return (floats * inverse, inverse)


def unit_backward(unit_rows, inverse, upstream):
    return inverse * (upstream - unit_rows * jnp.sum(unit_rows * upstream, axis=-1, keepdims=True))


def place(wide_count, wide_step, narrow_index):
    return (lax.rem(lax.axis_index("wide") + wide_step + wide_count, wide_count), narrow_index)


def greet(neighbours):
    barrier = pltpu.get_barrier_semaphore()
    for neighbour in neighbours:
        pl.semaphore_signal(barrier, inc=1, device_id=neighbour, device_id_type=MESH)
    return barrier


def probability(own, visitor, temper, offset):
    scores = lax.dot_general(
        own, visitor, (((1,), (1,)), ((), ())), preferred_element_type=jnp.float32
    )
    return jax.nn.sigmoid(temper * scores + offset)


def pull(own, visitor, temper, offset):
    weighted = (temper * probability(own, visitor, temper, offset)).astype(jnp.bfloat16)
    return jnp.dot(weighted, visitor, preferred_element_type=jnp.float32)


def own_pairs(image_rows, text_rows, labels_row, anchor, temper, offset):
    rows = image_rows.shape[0]
    target = anchor * rows + lax.broadcasted_iota(jnp.int32, (rows, rows), 0)
    positive = (labels_row == target).astype(jnp.float32)
    residual = probability(text_rows, image_rows, temper, offset) - positive
    weighted = (temper * residual).astype(jnp.bfloat16)
    image_grad = lax.dot_general(
        weighted, text_rows, (((0,), (0,)), ((), ())), preferred_element_type=jnp.float32
    )
    return image_grad, jnp.dot(weighted, image_rows, preferred_element_type=jnp.float32)


IMAGE, TEXT, IMAGE_ACROSS, TEXT_BACK = range(4)
I0, I1, I2, I3, T0, T1, T4, T5 = range(8)


def relay_kernel(
    wide_count,
    narrow_count,
    log_scale_ref,
    bias_ref,
    images_ref,
    texts_ref,
    labels_ref,
    grad_images_ref,
    grad_texts_ref,
    raw,
    labels_row,
    blocks,
    grads,
    outbox,
    inbox,
    load_sem,
    send_sem,
    recv_sem,
    grad_send_sem,
    grad_recv_sem,
):
    rows = blocks.shape[1]
    piece = rows // CHUNKS
    half = CHUNKS // 2
    narrow = lax.axis_index("narrow")
    partner = place(wide_count, 0, narrow + 1 - 2 * lax.rem(narrow, 2))
    across = place(wide_count, 0, lax.rem(narrow + 2, narrow_count))
    forth = place(wide_count, 1, narrow)
    back = place(wide_count, -1, narrow)
    neighbours = [partner, across, forth, back]

    def part(chunk):
        return pl.ds(chunk * piece, piece)

    sources = ((I0, raw.at[IMAGE], images_ref), (T0, raw.at[TEXT], texts_ref))
    loads = [
        [
            pltpu.make_async_copy(ref.at[part(chunk)], target.at[part(chunk)], load_sem.at[number, chunk])
            for number, (_, target, ref) in enumerate(sources)
        ]
        for chunk in range(CHUNKS)
    ]
    for pair in loads:
        for load in pair:
            load.start()
    label_load = pltpu.make_async_copy(labels_ref, labels_row, load_sem.at[2, 0])
    label_load.start()
    barrier = greet(neighbours)

    temper = jnp.exp(jnp.full((1, 1), log_scale_ref[0], jnp.float32))
    offset = bias_ref[0]
    started = []

    def message(source, slot, chunk, target):
        return pltpu.make_async_remote_copy(
            src_ref=blocks.at[source, part(chunk)],
            dst_ref=blocks.at[slot, part(chunk)],
            send_sem=send_sem.at[slot, chunk],
            recv_sem=recv_sem.at[slot, chunk],
            device_id=target,
            device_id_type=MESH,
        )

    def send(source, slot, chunk, target):
        copy = message(source, slot, chunk, target)
        copy.start()
        started.append(copy)

    def arrived(slot, first=0, last=CHUNKS):
        for chunk in range(first, last):
            message(slot, slot, chunk, partner).wait_recv()

    def return_message(side, chunk):
        return pltpu.make_async_remote_copy(
            src_ref=outbox.at[side, part(chunk)],
            dst_ref=inbox.at[side, part(chunk)],
            send_sem=grad_send_sem.at[side, chunk],
            recv_sem=grad_recv_sem.at[side, chunk],
            device_id=back if side else across,
            device_id_type=MESH,
        )

    for chunk in range(CHUNKS):
        for load in loads[chunk]:
            load.wait()
        for slot, source, _ in sources:
            unit, _ = normalize(source[part(chunk), :])
            blocks[slot, part(chunk), :] = unit.astype(jnp.bfloat16)
        if chunk == 0:
            pl.semaphore_wait(barrier, len(neighbours))
        send(I0, I2, chunk, across)
        send(T0, T4, chunk, forth)
        send(I0, I1, chunk, partner)
        send(T0, T1, chunk, partner)

    def cut(half_or_all):
        return slice(None) if half_or_all is None else pl.ds(half_or_all * half * piece, half * piece)

    def add(target, own, own_half, first, rows_of_each=slice(None), count=2, fresh=False):
        visitor = blocks[first : first + count, rows_of_each, :]
        visitor = visitor.reshape(visitor.shape[0] * visitor.shape[1], visitor.shape[2])
        value = pull(blocks[own, cut(own_half), :], visitor, temper, offset)
        grads[target, cut(own_half), :] = value if fresh else grads[target, cut(own_half), :] + value

    def pass_on(chunk):
        arrived(T4, chunk, chunk + 1)
        send(T4, T5, chunk, partner)
        arrived(I2, chunk, chunk + 1)
        send(I2, I3, chunk, partner)

    def give(side, own_half):
        target = TEXT_BACK if side else IMAGE_ACROSS
        for chunk in range(own_half * half, (own_half + 1) * half):
            outbox[side, part(chunk), :] = grads[target, part(chunk), :].astype(outbox.dtype)
            copy = return_message(side, chunk)
            copy.start()
            started.append(copy)

    label_load.wait()
    anchor = lax.axis_index("wide") * narrow_count + narrow
    grads[IMAGE], grads[TEXT] = own_pairs(
        blocks[I0], blocks[T0], labels_row[...], anchor, temper, offset
    )
    arrived(I1)
    arrived(T1)
    add(IMAGE, I0, None, T1, count=1)
    add(TEXT, T0, None, I1, count=1)

    for chunk in range(half):
        pass_on(chunk)
    add(IMAGE_ACROSS, I2, 0, T0, fresh=True)
    add(TEXT_BACK, T4, 0, I0, fresh=True)
    arrived(T5, 0, half)
    add(IMAGE_ACROSS, I2, 0, T4, cut(0))
    arrived(I3, 0, half)
    add(TEXT_BACK, T4, 0, I2, cut(0))
    for chunk in range(half, CHUNKS):
        pass_on(chunk)
        arrived(T5, chunk, chunk + 1)
        add(IMAGE_ACROSS, I2, 0, T4, part(chunk))
        if chunk == CHUNKS - 1:
            give(IMAGE, 0)
        arrived(I3, chunk, chunk + 1)
        add(TEXT_BACK, T4, 0, I2, part(chunk))
    give(TEXT, 0)
    add(IMAGE_ACROSS, I2, 1, T0, count=4, fresh=True)
    give(IMAGE, 1)
    add(TEXT_BACK, T4, 1, I0, count=4, fresh=True)
    give(TEXT, 1)
    add(IMAGE, I0, None, T4)
    add(TEXT, T0, None, I2)

    for chunk in range(CHUNKS):
        for side, out in ((IMAGE, grad_images_ref), (TEXT, grad_texts_ref)):
            return_message(side, chunk).wait_recv()
            unit, inverse = normalize(raw[side, part(chunk), :])
            total = grads[side, part(chunk), :] + inbox[side, part(chunk), :].astype(jnp.float32)
            out[part(chunk), :] = unit_backward(unit, inverse, total)
    for copy in started:
        copy.wait_send()


def direct_kernel(
    wide_count,
    narrow_count,
    log_scale_ref,
    bias_ref,
    images_ref,
    texts_ref,
    labels_ref,
    grad_images_ref,
    grad_texts_ref,
    labels_row,
    blocks,
    grads,
    load_sem,
    send_sem,
    recv_sem,
):
    rows = blocks.shape[2]
    wide = lax.axis_index("wide")
    narrow = lax.axis_index("narrow")
    slots = 2 * WINDOW
    targets = {}
    for side, sign in ((IMAGE, -1), (TEXT, 1)):
        for slot in range(1, slots):
            wide_back = slot // WINDOW
            narrow_back = slot - wide_back * WINDOW + wide_back * (WINDOW - 1)
            index = lax.rem(narrow + sign * narrow_back + 2 * narrow_count, narrow_count)
            targets[side, slot] = place(wide_count, sign * wide_back, index)
    load = pltpu.make_async_copy(labels_ref, labels_row, load_sem.at[0])
    load.start()
    barrier = greet(targets.values())

    temper = jnp.exp(jnp.full((1, 1), log_scale_ref[0], jnp.float32))
    offset = bias_ref[0]
    sources = {IMAGE: images_ref, TEXT: texts_ref}
    for side in (IMAGE, TEXT):
        blocks[side, 0] = normalize(sources[side][...])[0].astype(jnp.bfloat16)
    pl.semaphore_wait(barrier, len(targets))
    copies = {}
    for slot in range(1, slots):
        for side in (IMAGE, TEXT):
            copies[side, slot] = pltpu.make_async_remote_copy(
                src_ref=blocks.at[side, 0],
                dst_ref=blocks.at[side, slot],
                send_sem=send_sem.at[side, slot],
                recv_sem=recv_sem.at[side, slot],
                device_id=targets[side, slot],
                device_id_type=MESH,
            )
            copies[side, slot].start()
    load.wait()
    grads[IMAGE], grads[TEXT] = own_pairs(
        blocks[IMAGE, 0], blocks[TEXT, 0], labels_row[...], wide * narrow_count + narrow, temper, offset
    )
    for copy in copies.values():
        copy.wait_recv()

    @pl.loop(2, 2 * slots)
    def _(step):
        side = lax.rem(step, 2)
        grads[1 - side] += pull(blocks[1 - side, 0], blocks[side, step // 2], temper, offset)

    for side, out in ((IMAGE, grad_images_ref), (TEXT, grad_texts_ref)):
        unit, inverse = normalize(sources[side][...])
        out[...] = unit_backward(unit, inverse, grads[side])
    for copy in copies.values():
        copy.wait_send()


def shards(images, texts, labels, log_scale, bias):
    rows, depth = images.shape
    wide_count = lax.axis_size("wide")
    narrow_count = lax.axis_size("narrow")
    vmem = pl.BlockSpec(memory_space=pltpu.VMEM)
    smem = pl.BlockSpec(memory_space=pltpu.SMEM)
    hbm = pl.BlockSpec(memory_space=pltpu.HBM)
    row = pltpu.VMEM((1, rows), jnp.int32)
    dma = pltpu.SemaphoreType.DMA
    out = jax.ShapeDtypeStruct((rows, depth), jnp.float32)
    pairs = 2 * 2 * WINDOW * rows * rows
    if narrow_count == WINDOW:
        body, held = relay_kernel, hbm
        scratch = [
            pltpu.VMEM((2, rows, depth), images.dtype),
            row,
            pltpu.VMEM((2 * WINDOW, rows, depth), jnp.bfloat16),
            pltpu.VMEM((4, rows, depth), jnp.float32),
            pltpu.VMEM((2, rows, depth), jnp.bfloat16),
            pltpu.VMEM((2, rows, depth), jnp.bfloat16),
            dma((3, CHUNKS)),
            dma((2 * WINDOW, CHUNKS)),
            dma((2 * WINDOW, CHUNKS)),
            dma((2, CHUNKS)),
            dma((2, CHUNKS)),
        ]
    else:
        body, held = direct_kernel, vmem
        scratch = [
            row,
            pltpu.VMEM((2, 2 * WINDOW, rows, depth), jnp.bfloat16),
            pltpu.VMEM((2, rows, depth), jnp.float32),
            dma((1,)),
            dma((2, 2 * WINDOW)),
            dma((2, 2 * WINDOW)),
        ]
    arrays = (images, texts, labels.reshape(1, rows))
    if held is hbm:
        arrays = tuple(pltpu.with_memory_space_constraint(array, pltpu.HBM) for array in arrays)
    return pl.pallas_call(
        functools.partial(body, wide_count, narrow_count),
        out_shape=(out, out),
        in_specs=[smem, smem, held, held, hbm],
        out_specs=(vmem, vmem),
        scratch_shapes=scratch,
        compiler_params=pltpu.CompilerParams(
            collective_id=0, has_side_effects=True, vmem_limit_bytes=40 * 1024 * 1024
        ),
        cost_estimate=pl.CostEstimate(
            flops=4 * pairs * depth, bytes_accessed=12 * rows * depth, transcendentals=pairs
        ),
        name="window_grads",
    )(log_scale, bias, *arrays)

def solution(mesh):
    return jax.shard_map(
        shards,
        mesh=mesh,
        in_specs=(
            P(("wide", "narrow"), None),
            P(("wide", "narrow"), None),
            P(("wide", "narrow")),
            P(),
            P(),
        ),
        out_specs=(P(("wide", "narrow"), None), P(("wide", "narrow"), None)),
        check_vma=False,
    )
```

```python
import functools

import jax
import jax.numpy as jnp
from jax import lax
from jax.experimental import pallas as pl
from jax.experimental.pallas import tpu as pltpu
from jax.sharding import PartitionSpec as P

WINDOW = 4
EPS = 1e-06
CHUNKS = 4
MESH = pl.DeviceIdType.MESH


def normalize(vectors):
    floats = vectors.astype(jnp.float32)
    inverse = lax.rsqrt(jnp.sum(floats * floats, axis=-1, keepdims=True) + EPS)
    return (floats * inverse, inverse)


def unit_backward(unit_rows, inverse, upstream):
    return inverse * (upstream - unit_rows * jnp.sum(unit_rows * upstream, axis=-1, keepdims=True))


def place(wide_count, wide_step, narrow_index):
    return (lax.rem(lax.axis_index("wide") + wide_step + wide_count, wide_count), narrow_index)


def greet(neighbours):
    barrier = pltpu.get_barrier_semaphore()
    for neighbour in neighbours:
        pl.semaphore_signal(barrier, inc=1, device_id=neighbour, device_id_type=MESH)
    return barrier


def probability(own, visitor, temper, offset):
    scores = lax.dot_general(
        own, visitor, (((1,), (1,)), ((), ())), preferred_element_type=jnp.float32
    )
    return jax.nn.sigmoid(temper * scores + offset)


def pull(own, visitor, temper, offset):
    weighted = (temper * probability(own, visitor, temper, offset)).astype(jnp.bfloat16)
    return jnp.dot(weighted, visitor, preferred_element_type=jnp.float32)


def own_pairs(image_rows, text_rows, labels_row, anchor, temper, offset):
    rows = image_rows.shape[0]
    target = anchor * rows + lax.broadcasted_iota(jnp.int32, (rows, rows), 0)
    positive = (labels_row == target).astype(jnp.float32)
    residual = probability(text_rows, image_rows, temper, offset) - positive
    weighted = (temper * residual).astype(jnp.bfloat16)
    image_grad = lax.dot_general(
        weighted, text_rows, (((0,), (0,)), ((), ())), preferred_element_type=jnp.float32
    )
    return image_grad, jnp.dot(weighted, image_rows, preferred_element_type=jnp.float32)


IMAGE, TEXT, IMAGE_ACROSS, TEXT_BACK = range(4)
I0, I1, I2, I3, T0, T1, T4, T5 = range(8)


def relay_kernel(
    wide_count,
    narrow_count,
    log_scale_ref,
    bias_ref,
    images_ref,
    texts_ref,
    labels_ref,
    grad_images_ref,
    grad_texts_ref,
    raw,
    labels_row,
    blocks,
    grads,
    outbox,
    inbox,
    load_sem,
    send_sem,
    recv_sem,
    grad_send_sem,
    grad_recv_sem,
):
    rows = blocks.shape[1]
    piece = rows // CHUNKS
    half = CHUNKS // 2
    narrow = lax.axis_index("narrow")
    partner = place(wide_count, 0, narrow + 1 - 2 * lax.rem(narrow, 2))
    across = place(wide_count, 0, lax.rem(narrow + 2, narrow_count))
    forth = place(wide_count, 1, narrow)
    back = place(wide_count, -1, narrow)
    neighbours = [partner, across, forth, back]

    def part(chunk):
        return pl.ds(chunk * piece, piece)

    sources = ((I0, raw.at[IMAGE], images_ref), (T0, raw.at[TEXT], texts_ref))
    loads = [
        [
            pltpu.make_async_copy(ref.at[part(chunk)], target.at[part(chunk)], load_sem.at[number, chunk])
            for number, (_, target, ref) in enumerate(sources)
        ]
        for chunk in range(CHUNKS)
    ]
    for pair in loads:
        for load in pair:
            load.start()
    label_load = pltpu.make_async_copy(labels_ref, labels_row, load_sem.at[2, 0])
    label_load.start()
    barrier = greet(neighbours)

    temper = jnp.exp(jnp.full((1, 1), log_scale_ref[0], jnp.float32))
    offset = bias_ref[0]
    started = []

    def message(source, slot, chunk, target):
        return pltpu.make_async_remote_copy(
            src_ref=blocks.at[source, part(chunk)],
            dst_ref=blocks.at[slot, part(chunk)],
            send_sem=send_sem.at[slot, chunk],
            recv_sem=recv_sem.at[slot, chunk],
            device_id=target,
            device_id_type=MESH,
        )

    def send(source, slot, chunk, target):
        copy = message(source, slot, chunk, target)
        copy.start()
        started.append(copy)

    def whole(source, slot):
        return pltpu.make_async_remote_copy(
            src_ref=blocks.at[source],
            dst_ref=blocks.at[slot],
            send_sem=send_sem.at[slot, 0],
            recv_sem=recv_sem.at[slot, 0],
            device_id=partner,
            device_id_type=MESH,
        )

    def arrived(slot, first, last):
        for chunk in range(first, last):
            message(slot, slot, chunk, partner).wait_recv()

    def return_message(side, chunk):
        return pltpu.make_async_remote_copy(
            src_ref=outbox.at[side, part(chunk)],
            dst_ref=inbox.at[side, part(chunk)],
            send_sem=grad_send_sem.at[side, chunk],
            recv_sem=grad_recv_sem.at[side, chunk],
            device_id=back if side else across,
            device_id_type=MESH,
        )

    for chunk in range(CHUNKS):
        for load in loads[chunk]:
            load.wait()
        for slot, source, _ in sources:
            unit, _ = normalize(source[part(chunk), :])
            blocks[slot, part(chunk), :] = unit.astype(jnp.bfloat16)
        if chunk == 0:
            pl.semaphore_wait(barrier, len(neighbours))
        send(I0, I2, chunk, across)
        send(T0, T4, chunk, forth)
    for slot, source in ((I1, I0), (T1, T0)):
        started.append(whole(source, slot))
        started[-1].start()

    def cut(half_or_all):
        return slice(None) if half_or_all is None else pl.ds(half_or_all * half * piece, half * piece)

    def add(target, own, own_half, first, rows_of_each=slice(None), count=2, fresh=False):
        visitor = blocks[first : first + count, rows_of_each, :]
        visitor = visitor.reshape(visitor.shape[0] * visitor.shape[1], visitor.shape[2])
        value = pull(blocks[own, cut(own_half), :], visitor, temper, offset)
        grads[target, cut(own_half), :] = value if fresh else grads[target, cut(own_half), :] + value

    def pass_on(chunk):
        arrived(T4, chunk, chunk + 1)
        send(T4, T5, chunk, partner)
        arrived(I2, chunk, chunk + 1)
        send(I2, I3, chunk, partner)

    def give(side, own_half):
        target = TEXT_BACK if side else IMAGE_ACROSS
        for chunk in range(own_half * half, (own_half + 1) * half):
            outbox[side, part(chunk), :] = grads[target, part(chunk), :].astype(outbox.dtype)
            copy = return_message(side, chunk)
            copy.start()
            started.append(copy)

    label_load.wait()
    anchor = lax.axis_index("wide") * narrow_count + narrow
    grads[IMAGE], grads[TEXT] = own_pairs(
        blocks[I0], blocks[T0], labels_row[...], anchor, temper, offset
    )
    whole(I0, I1).wait_recv()
    whole(T0, T1).wait_recv()
    add(IMAGE, I0, None, T1, count=1)
    add(TEXT, T0, None, I1, count=1)

    for chunk in range(half):
        pass_on(chunk)
    add(IMAGE_ACROSS, I2, 0, T0, fresh=True)
    add(TEXT_BACK, T4, 0, I0, fresh=True)
    arrived(T5, 0, half)
    add(IMAGE_ACROSS, I2, 0, T4, cut(0))
    arrived(I3, 0, half)
    add(TEXT_BACK, T4, 0, I2, cut(0))
    for chunk in range(half, CHUNKS):
        pass_on(chunk)
        arrived(T5, chunk, chunk + 1)
        add(IMAGE_ACROSS, I2, 0, T4, part(chunk))
        if chunk == CHUNKS - 1:
            give(IMAGE, 0)
        arrived(I3, chunk, chunk + 1)
        add(TEXT_BACK, T4, 0, I2, part(chunk))
    give(TEXT, 0)
    add(IMAGE_ACROSS, I2, 1, T0, count=4, fresh=True)
    give(IMAGE, 1)
    add(TEXT_BACK, T4, 1, I0, count=4, fresh=True)
    give(TEXT, 1)
    add(IMAGE, I0, None, T4)
    add(TEXT, T0, None, I2)

    for chunk in range(CHUNKS):
        for side, out in ((IMAGE, grad_images_ref), (TEXT, grad_texts_ref)):
            return_message(side, chunk).wait_recv()
            unit, inverse = normalize(raw[side, part(chunk), :])
            total = grads[side, part(chunk), :] + inbox[side, part(chunk), :].astype(jnp.float32)
            out[part(chunk), :] = unit_backward(unit, inverse, total)
    for copy in started:
        copy.wait_send()


def direct_kernel(
    wide_count,
    narrow_count,
    log_scale_ref,
    bias_ref,
    images_ref,
    texts_ref,
    labels_ref,
    grad_images_ref,
    grad_texts_ref,
    labels_row,
    blocks,
    grads,
    load_sem,
    send_sem,
    recv_sem,
):
    rows = blocks.shape[2]
    wide = lax.axis_index("wide")
    narrow = lax.axis_index("narrow")
    slots = 2 * WINDOW
    targets = {}
    for side, sign in ((IMAGE, -1), (TEXT, 1)):
        for slot in range(1, slots):
            wide_back = slot // WINDOW
            narrow_back = slot - wide_back * WINDOW + wide_back * (WINDOW - 1)
            index = lax.rem(narrow + sign * narrow_back + 2 * narrow_count, narrow_count)
            targets[side, slot] = place(wide_count, sign * wide_back, index)
    load = pltpu.make_async_copy(labels_ref, labels_row, load_sem.at[0])
    load.start()
    barrier = greet(targets.values())

    temper = jnp.exp(jnp.full((1, 1), log_scale_ref[0], jnp.float32))
    offset = bias_ref[0]
    sources = {IMAGE: images_ref, TEXT: texts_ref}
    for side in (IMAGE, TEXT):
        blocks[side, 0] = normalize(sources[side][...])[0].astype(jnp.bfloat16)
    pl.semaphore_wait(barrier, len(targets))
    copies = {}
    for slot in range(1, slots):
        for side in (IMAGE, TEXT):
            copies[side, slot] = pltpu.make_async_remote_copy(
                src_ref=blocks.at[side, 0],
                dst_ref=blocks.at[side, slot],
                send_sem=send_sem.at[side, slot],
                recv_sem=recv_sem.at[side, slot],
                device_id=targets[side, slot],
                device_id_type=MESH,
            )
            copies[side, slot].start()
    load.wait()
    grads[IMAGE], grads[TEXT] = own_pairs(
        blocks[IMAGE, 0], blocks[TEXT, 0], labels_row[...], wide * narrow_count + narrow, temper, offset
    )
    for copy in copies.values():
        copy.wait_recv()

    @pl.loop(2, 2 * slots)
    def _(step):
        side = lax.rem(step, 2)
        grads[1 - side] += pull(blocks[1 - side, 0], blocks[side, step // 2], temper, offset)

    for side, out in ((IMAGE, grad_images_ref), (TEXT, grad_texts_ref)):
        unit, inverse = normalize(sources[side][...])
        out[...] = unit_backward(unit, inverse, grads[side])
    for copy in copies.values():
        copy.wait_send()


def shards(images, texts, labels, log_scale, bias):
    rows, depth = images.shape
    wide_count = lax.axis_size("wide")
    narrow_count = lax.axis_size("narrow")
    vmem = pl.BlockSpec(memory_space=pltpu.VMEM)
    smem = pl.BlockSpec(memory_space=pltpu.SMEM)
    hbm = pl.BlockSpec(memory_space=pltpu.HBM)
    row = pltpu.VMEM((1, rows), jnp.int32)
    dma = pltpu.SemaphoreType.DMA
    out = jax.ShapeDtypeStruct((rows, depth), jnp.float32)
    pairs = 2 * 2 * WINDOW * rows * rows
    if narrow_count == WINDOW:
        body, held = relay_kernel, hbm
        scratch = [
            pltpu.VMEM((2, rows, depth), images.dtype),
            row,
            pltpu.VMEM((2 * WINDOW, rows, depth), jnp.bfloat16),
            pltpu.VMEM((4, rows, depth), jnp.float32),
            pltpu.VMEM((2, rows, depth), jnp.bfloat16),
            pltpu.VMEM((2, rows, depth), jnp.bfloat16),
            dma((3, CHUNKS)),
            dma((2 * WINDOW, CHUNKS)),
            dma((2 * WINDOW, CHUNKS)),
            dma((2, CHUNKS)),
            dma((2, CHUNKS)),
        ]
    else:
        body, held = direct_kernel, vmem
        scratch = [
            row,
            pltpu.VMEM((2, 2 * WINDOW, rows, depth), jnp.bfloat16),
            pltpu.VMEM((2, rows, depth), jnp.float32),
            dma((1,)),
            dma((2, 2 * WINDOW)),
            dma((2, 2 * WINDOW)),
        ]
    arrays = (images, texts, labels.reshape(1, rows))
    if held is hbm:
        arrays = tuple(pltpu.with_memory_space_constraint(array, pltpu.HBM) for array in arrays)
    return pl.pallas_call(
        functools.partial(body, wide_count, narrow_count),
        out_shape=(out, out),
        in_specs=[smem, smem, held, held, hbm],
        out_specs=(vmem, vmem),
        scratch_shapes=scratch,
        compiler_params=pltpu.CompilerParams(
            collective_id=0, has_side_effects=True, vmem_limit_bytes=40 * 1024 * 1024
        ),
        cost_estimate=pl.CostEstimate(
            flops=4 * pairs * depth, bytes_accessed=12 * rows * depth, transcendentals=pairs
        ),
        name="window_grads",
    )(log_scale, bias, *arrays)

def solution(mesh):
    return jax.shard_map(
        shards,
        mesh=mesh,
        in_specs=(
            P(("wide", "narrow"), None),
            P(("wide", "narrow"), None),
            P(("wide", "narrow")),
            P(),
            P(),
        ),
        out_specs=(P(("wide", "narrow"), None), P(("wide", "narrow"), None)),
        check_vma=False,
    )
```

```python
import functools

import jax
import jax.numpy as jnp
from jax import lax
from jax.experimental import pallas as pl
from jax.experimental.pallas import tpu as pltpu
from jax.sharding import PartitionSpec as P

WINDOW = 4
EPS = 1e-06
CHUNKS = 4
MESH = pl.DeviceIdType.MESH


def normalize(vectors):
    floats = vectors.astype(jnp.float32)
    inverse = lax.rsqrt(jnp.sum(floats * floats, axis=-1, keepdims=True) + EPS)
    return (floats * inverse, inverse)


def unit_backward(unit_rows, inverse, upstream):
    return inverse * (upstream - unit_rows * jnp.sum(unit_rows * upstream, axis=-1, keepdims=True))


def place(wide_count, wide_step, narrow_index):
    return (lax.rem(lax.axis_index("wide") + wide_step + wide_count, wide_count), narrow_index)


def greet(neighbours):
    barrier = pltpu.get_barrier_semaphore()
    for neighbour in neighbours:
        pl.semaphore_signal(barrier, inc=1, device_id=neighbour, device_id_type=MESH)
    return barrier


def probability(own, visitor, temper, offset):
    scores = lax.dot_general(
        own, visitor, (((1,), (1,)), ((), ())), preferred_element_type=jnp.float32
    )
    return jax.nn.sigmoid(temper * scores + offset)


def pull(own, visitor, temper, offset):
    weighted = (temper * probability(own, visitor, temper, offset)).astype(jnp.bfloat16)
    return jnp.dot(weighted, visitor, preferred_element_type=jnp.float32)


def own_pairs(image_rows, text_rows, labels_row, anchor, temper, offset):
    rows = image_rows.shape[0]
    target = anchor * rows + lax.broadcasted_iota(jnp.int32, (rows, rows), 0)
    positive = (labels_row == target).astype(jnp.float32)
    residual = probability(text_rows, image_rows, temper, offset) - positive
    weighted = (temper * residual).astype(jnp.bfloat16)
    image_grad = lax.dot_general(
        weighted, text_rows, (((0,), (0,)), ((), ())), preferred_element_type=jnp.float32
    )
    return image_grad, jnp.dot(weighted, image_rows, preferred_element_type=jnp.float32)


IMAGE, TEXT, IMAGE_ACROSS, TEXT_BACK = range(4)
I0, I1, I2, I3, T0, T1, T4, T5 = range(8)


def relay_kernel(
    wide_count,
    narrow_count,
    log_scale_ref,
    bias_ref,
    images_ref,
    texts_ref,
    labels_ref,
    grad_images_ref,
    grad_texts_ref,
    raw,
    labels_row,
    blocks,
    grads,
    outbox,
    inbox,
    load_sem,
    send_sem,
    recv_sem,
    grad_send_sem,
    grad_recv_sem,
):
    rows = blocks.shape[1]
    piece = rows // CHUNKS
    half = CHUNKS // 2
    narrow = lax.axis_index("narrow")
    partner = place(wide_count, 0, narrow + 1 - 2 * lax.rem(narrow, 2))
    across = place(wide_count, 0, lax.rem(narrow + 2, narrow_count))
    forth = place(wide_count, 1, narrow)
    back = place(wide_count, -1, narrow)
    neighbours = [partner, across, forth, back]

    def part(chunk):
        return pl.ds(chunk * piece, piece)

    sources = ((I0, raw.at[IMAGE], images_ref), (T0, raw.at[TEXT], texts_ref))
    loads = [
        [
            pltpu.make_async_copy(ref.at[part(chunk)], target.at[part(chunk)], load_sem.at[number, chunk])
            for number, (_, target, ref) in enumerate(sources)
        ]
        for chunk in range(CHUNKS)
    ]
    for pair in loads:
        for load in pair:
            load.start()
    label_load = pltpu.make_async_copy(labels_ref, labels_row, load_sem.at[2, 0])
    label_load.start()
    barrier = greet(neighbours)

    temper = jnp.exp(jnp.full((1, 1), log_scale_ref[0], jnp.float32))
    offset = bias_ref[0]
    started = []

    def message(source, slot, chunk, target):
        return pltpu.make_async_remote_copy(
            src_ref=blocks.at[source, part(chunk)],
            dst_ref=blocks.at[slot, part(chunk)],
            send_sem=send_sem.at[slot, chunk],
            recv_sem=recv_sem.at[slot, chunk],
            device_id=target,
            device_id_type=MESH,
        )

    def send(source, slot, chunk, target):
        copy = message(source, slot, chunk, target)
        copy.start()
        started.append(copy)

    def whole(source, slot):
        return pltpu.make_async_remote_copy(
            src_ref=blocks.at[source],
            dst_ref=blocks.at[slot],
            send_sem=send_sem.at[slot, 0],
            recv_sem=recv_sem.at[slot, 0],
            device_id=partner,
            device_id_type=MESH,
        )

    def arrived(slot, first, last):
        for chunk in range(first, last):
            message(slot, slot, chunk, partner).wait_recv()

    def return_message(side, chunk):
        return pltpu.make_async_remote_copy(
            src_ref=outbox.at[side, part(chunk)],
            dst_ref=inbox.at[side, part(chunk)],
            send_sem=grad_send_sem.at[side, chunk],
            recv_sem=grad_recv_sem.at[side, chunk],
            device_id=back if side else across,
            device_id_type=MESH,
        )

    for chunk in range(CHUNKS):
        for load in loads[chunk]:
            load.wait()
        for slot, source, _ in sources:
            unit, _ = normalize(source[part(chunk), :])
            blocks[slot, part(chunk), :] = unit.astype(jnp.bfloat16)
        if chunk == 0:
            pl.semaphore_wait(barrier, len(neighbours))
        send(I0, I2, chunk, across)
        send(T0, T4, chunk, forth)
    for slot, source in ((I1, I0), (T1, T0)):
        started.append(whole(source, slot))
        started[-1].start()

    def cut(half_or_all):
        return slice(None) if half_or_all is None else pl.ds(half_or_all * half * piece, half * piece)

    def add(target, own, own_half, first, rows_of_each=slice(None), count=2, fresh=False):
        visitor = blocks[first : first + count, rows_of_each, :]
        visitor = visitor.reshape(visitor.shape[0] * visitor.shape[1], visitor.shape[2])
        value = pull(blocks[own, cut(own_half), :], visitor, temper, offset)
        grads[target, cut(own_half), :] = value if fresh else grads[target, cut(own_half), :] + value

    def pass_on(chunk):
        arrived(T4, chunk, chunk + 1)
        send(T4, T5, chunk, partner)
        arrived(I2, chunk, chunk + 1)
        send(I2, I3, chunk, partner)

    def last_adds(own_half, rows_of_each, first_image, first_text, count, fresh):
        totals = []
        for target, own, first in ((IMAGE_ACROSS, I2, first_text), (TEXT_BACK, T4, first_image)):
            visitor = blocks[first : first + count, rows_of_each, :]
            visitor = visitor.reshape(visitor.shape[0] * visitor.shape[1], visitor.shape[2])
            value = pull(blocks[own, cut(own_half), :], visitor, temper, offset)
            totals.append(value if fresh else grads[target, cut(own_half), :] + value)
        for side, total in enumerate(totals):
            outbox[side, cut(own_half), :] = total.astype(outbox.dtype)
        for chunk in range(own_half * half, (own_half + 1) * half):
            for side in (IMAGE, TEXT):
                copy = return_message(side, chunk)
                copy.start()
                started.append(copy)

    label_load.wait()
    anchor = lax.axis_index("wide") * narrow_count + narrow
    grads[IMAGE], grads[TEXT] = own_pairs(
        blocks[I0], blocks[T0], labels_row[...], anchor, temper, offset
    )
    whole(I0, I1).wait_recv()
    whole(T0, T1).wait_recv()
    add(IMAGE, I0, None, T1, count=1)
    add(TEXT, T0, None, I1, count=1)

    for chunk in range(half):
        pass_on(chunk)
    add(IMAGE_ACROSS, I2, 0, T0, fresh=True)
    add(TEXT_BACK, T4, 0, I0, fresh=True)
    arrived(T5, 0, half)
    add(IMAGE_ACROSS, I2, 0, T4, cut(0))
    arrived(I3, 0, half)
    add(TEXT_BACK, T4, 0, I2, cut(0))
    for chunk in range(half, CHUNKS):
        pass_on(chunk)
        arrived(T5, chunk, chunk + 1)
        arrived(I3, chunk, chunk + 1)
        if chunk < CHUNKS - 1:
            add(IMAGE_ACROSS, I2, 0, T4, part(chunk))
            add(TEXT_BACK, T4, 0, I2, part(chunk))
    last_adds(0, part(CHUNKS - 1), I2, T4, 2, False)
    last_adds(1, slice(None), I0, T0, 4, True)
    add(IMAGE, I0, None, T4)
    add(TEXT, T0, None, I2)

    for chunk in range(CHUNKS):
        for side, out in ((IMAGE, grad_images_ref), (TEXT, grad_texts_ref)):
            return_message(side, chunk).wait_recv()
            unit, inverse = normalize(raw[side, part(chunk), :])
            total = grads[side, part(chunk), :] + inbox[side, part(chunk), :].astype(jnp.float32)
            out[part(chunk), :] = unit_backward(unit, inverse, total)
    for copy in started:
        copy.wait_send()


def direct_kernel(
    wide_count,
    narrow_count,
    log_scale_ref,
    bias_ref,
    images_ref,
    texts_ref,
    labels_ref,
    grad_images_ref,
    grad_texts_ref,
    labels_row,
    blocks,
    grads,
    load_sem,
    send_sem,
    recv_sem,
):
    rows = blocks.shape[2]
    wide = lax.axis_index("wide")
    narrow = lax.axis_index("narrow")
    slots = 2 * WINDOW
    targets = {}
    for side, sign in ((IMAGE, -1), (TEXT, 1)):
        for slot in range(1, slots):
            wide_back = slot // WINDOW
            narrow_back = slot - wide_back * WINDOW + wide_back * (WINDOW - 1)
            index = lax.rem(narrow + sign * narrow_back + 2 * narrow_count, narrow_count)
            targets[side, slot] = place(wide_count, sign * wide_back, index)
    load = pltpu.make_async_copy(labels_ref, labels_row, load_sem.at[0])
    load.start()
    barrier = greet(targets.values())

    temper = jnp.exp(jnp.full((1, 1), log_scale_ref[0], jnp.float32))
    offset = bias_ref[0]
    sources = {IMAGE: images_ref, TEXT: texts_ref}
    for side in (IMAGE, TEXT):
        blocks[side, 0] = normalize(sources[side][...])[0].astype(jnp.bfloat16)
    pl.semaphore_wait(barrier, len(targets))
    copies = {}
    for slot in range(1, slots):
        for side in (IMAGE, TEXT):
            copies[side, slot] = pltpu.make_async_remote_copy(
                src_ref=blocks.at[side, 0],
                dst_ref=blocks.at[side, slot],
                send_sem=send_sem.at[side, slot],
                recv_sem=recv_sem.at[side, slot],
                device_id=targets[side, slot],
                device_id_type=MESH,
            )
            copies[side, slot].start()
    load.wait()
    grads[IMAGE], grads[TEXT] = own_pairs(
        blocks[IMAGE, 0], blocks[TEXT, 0], labels_row[...], wide * narrow_count + narrow, temper, offset
    )
    for copy in copies.values():
        copy.wait_recv()

    @pl.loop(2, 2 * slots)
    def _(step):
        side = lax.rem(step, 2)
        grads[1 - side] += pull(blocks[1 - side, 0], blocks[side, step // 2], temper, offset)

    for side, out in ((IMAGE, grad_images_ref), (TEXT, grad_texts_ref)):
        unit, inverse = normalize(sources[side][...])
        out[...] = unit_backward(unit, inverse, grads[side])
    for copy in copies.values():
        copy.wait_send()


def shards(images, texts, labels, log_scale, bias):
    rows, depth = images.shape
    wide_count = lax.axis_size("wide")
    narrow_count = lax.axis_size("narrow")
    vmem = pl.BlockSpec(memory_space=pltpu.VMEM)
    smem = pl.BlockSpec(memory_space=pltpu.SMEM)
    hbm = pl.BlockSpec(memory_space=pltpu.HBM)
    row = pltpu.VMEM((1, rows), jnp.int32)
    dma = pltpu.SemaphoreType.DMA
    out = jax.ShapeDtypeStruct((rows, depth), jnp.float32)
    pairs = 2 * 2 * WINDOW * rows * rows
    if narrow_count == WINDOW:
        body, held = relay_kernel, hbm
        scratch = [
            pltpu.VMEM((2, rows, depth), images.dtype),
            row,
            pltpu.VMEM((2 * WINDOW, rows, depth), jnp.bfloat16),
            pltpu.VMEM((4, rows, depth), jnp.float32),
            pltpu.VMEM((2, rows, depth), jnp.bfloat16),
            pltpu.VMEM((2, rows, depth), jnp.bfloat16),
            dma((3, CHUNKS)),
            dma((2 * WINDOW, CHUNKS)),
            dma((2 * WINDOW, CHUNKS)),
            dma((2, CHUNKS)),
            dma((2, CHUNKS)),
        ]
    else:
        body, held = direct_kernel, vmem
        scratch = [
            row,
            pltpu.VMEM((2, 2 * WINDOW, rows, depth), jnp.bfloat16),
            pltpu.VMEM((2, rows, depth), jnp.float32),
            dma((1,)),
            dma((2, 2 * WINDOW)),
            dma((2, 2 * WINDOW)),
        ]
    arrays = (images, texts, labels.reshape(1, rows))
    if held is hbm:
        arrays = tuple(pltpu.with_memory_space_constraint(array, pltpu.HBM) for array in arrays)
    return pl.pallas_call(
        functools.partial(body, wide_count, narrow_count),
        out_shape=(out, out),
        in_specs=[smem, smem, held, held, hbm],
        out_specs=(vmem, vmem),
        scratch_shapes=scratch,
        compiler_params=pltpu.CompilerParams(
            collective_id=0, has_side_effects=True, vmem_limit_bytes=40 * 1024 * 1024
        ),
        cost_estimate=pl.CostEstimate(
            flops=4 * pairs * depth, bytes_accessed=12 * rows * depth, transcendentals=pairs
        ),
        name="window_grads",
    )(log_scale, bias, *arrays)

def solution(mesh):
    return jax.shard_map(
        shards,
        mesh=mesh,
        in_specs=(
            P(("wide", "narrow"), None),
            P(("wide", "narrow"), None),
            P(("wide", "narrow")),
            P(),
            P(),
        ),
        out_specs=(P(("wide", "narrow"), None), P(("wide", "narrow"), None)),
        check_vma=False,
    )
```

```python
import functools

import jax
import jax.numpy as jnp
from jax import lax
from jax.experimental import pallas as pl
from jax.experimental.pallas import tpu as pltpu
from jax.sharding import PartitionSpec as P

WINDOW = 4
EPS = 1e-06
CHUNKS = 2
MESH = pl.DeviceIdType.MESH


def normalize(vectors):
    floats = vectors.astype(jnp.float32)
    inverse = lax.rsqrt(jnp.sum(floats * floats, axis=-1, keepdims=True) + EPS)
    return (floats * inverse, inverse)


def unit_backward(unit_rows, inverse, upstream):
    return inverse * (upstream - unit_rows * jnp.sum(unit_rows * upstream, axis=-1, keepdims=True))


def place(wide_count, wide_step, narrow_index):
    return (lax.rem(lax.axis_index("wide") + wide_step + wide_count, wide_count), narrow_index)


def greet(neighbours):
    barrier = pltpu.get_barrier_semaphore()
    for neighbour in neighbours:
        pl.semaphore_signal(barrier, inc=1, device_id=neighbour, device_id_type=MESH)
    return barrier


def probability(own, visitor, temper, offset):
    scores = lax.dot_general(
        own, visitor, (((1,), (1,)), ((), ())), preferred_element_type=jnp.float32
    )
    return jax.nn.sigmoid(temper * scores + offset)


def pull(own, visitor, temper, offset):
    weighted = (temper * probability(own, visitor, temper, offset)).astype(jnp.bfloat16)
    return jnp.dot(weighted, visitor, preferred_element_type=jnp.float32)


def own_pairs(image_rows, text_rows, labels_row, anchor, temper, offset):
    rows = image_rows.shape[0]
    target = anchor * rows + lax.broadcasted_iota(jnp.int32, (rows, rows), 0)
    positive = (labels_row == target).astype(jnp.float32)
    residual = probability(text_rows, image_rows, temper, offset) - positive
    weighted = (temper * residual).astype(jnp.bfloat16)
    image_grad = lax.dot_general(
        weighted, text_rows, (((0,), (0,)), ((), ())), preferred_element_type=jnp.float32
    )
    return image_grad, jnp.dot(weighted, image_rows, preferred_element_type=jnp.float32)


IMAGE, TEXT, IMAGE_ACROSS, TEXT_BACK = range(4)
I0, I1, I2, I3, T0, T1, T4, T5 = range(8)


def relay_kernel(
    wide_count,
    narrow_count,
    log_scale_ref,
    bias_ref,
    images_ref,
    texts_ref,
    labels_ref,
    grad_images_ref,
    grad_texts_ref,
    raw,
    labels_row,
    blocks,
    grads,
    outbox,
    inbox,
    load_sem,
    send_sem,
    recv_sem,
    grad_send_sem,
    grad_recv_sem,
):
    rows = blocks.shape[1]
    piece = rows // CHUNKS
    half = CHUNKS // 2
    narrow = lax.axis_index("narrow")
    partner = place(wide_count, 0, narrow + 1 - 2 * lax.rem(narrow, 2))
    across = place(wide_count, 0, lax.rem(narrow + 2, narrow_count))
    forth = place(wide_count, 1, narrow)
    back = place(wide_count, -1, narrow)
    neighbours = [partner, across, forth, back]

    def part(chunk):
        return pl.ds(chunk * piece, piece)

    sources = ((I0, raw.at[IMAGE], images_ref), (T0, raw.at[TEXT], texts_ref))
    loads = [
        [
            pltpu.make_async_copy(ref.at[part(chunk)], target.at[part(chunk)], load_sem.at[number, chunk])
            for number, (_, target, ref) in enumerate(sources)
        ]
        for chunk in range(CHUNKS)
    ]
    for pair in loads:
        for load in pair:
            load.start()
    label_load = pltpu.make_async_copy(labels_ref, labels_row, load_sem.at[2, 0])
    label_load.start()
    barrier = greet(neighbours)

    temper = jnp.exp(jnp.full((1, 1), log_scale_ref[0], jnp.float32))
    offset = bias_ref[0]
    started = []

    def message(source, slot, chunk, target):
        return pltpu.make_async_remote_copy(
            src_ref=blocks.at[source, part(chunk)],
            dst_ref=blocks.at[slot, part(chunk)],
            send_sem=send_sem.at[slot, chunk],
            recv_sem=recv_sem.at[slot, chunk],
            device_id=target,
            device_id_type=MESH,
        )

    def send(source, slot, chunk, target):
        copy = message(source, slot, chunk, target)
        copy.start()
        started.append(copy)

    def whole(source, slot):
        return pltpu.make_async_remote_copy(
            src_ref=blocks.at[source],
            dst_ref=blocks.at[slot],
            send_sem=send_sem.at[slot, 0],
            recv_sem=recv_sem.at[slot, 0],
            device_id=partner,
            device_id_type=MESH,
        )

    def arrived(slot, first, last):
        for chunk in range(first, last):
            message(slot, slot, chunk, partner).wait_recv()

    def return_message(side, chunk):
        return pltpu.make_async_remote_copy(
            src_ref=outbox.at[side, part(chunk)],
            dst_ref=inbox.at[side, part(chunk)],
            send_sem=grad_send_sem.at[side, chunk],
            recv_sem=grad_recv_sem.at[side, chunk],
            device_id=back if side else across,
            device_id_type=MESH,
        )

    for chunk in range(CHUNKS):
        for load in loads[chunk]:
            load.wait()
        for slot, source, _ in sources:
            unit, _ = normalize(source[part(chunk), :])
            blocks[slot, part(chunk), :] = unit.astype(jnp.bfloat16)
        if chunk == 0:
            pl.semaphore_wait(barrier, len(neighbours))
        send(I0, I2, chunk, across)
        send(T0, T4, chunk, forth)
    for slot, source in ((I1, I0), (T1, T0)):
        started.append(whole(source, slot))
        started[-1].start()

    def cut(half_or_all):
        return slice(None) if half_or_all is None else pl.ds(half_or_all * half * piece, half * piece)

    def add(target, own, own_half, first, rows_of_each=slice(None), count=2, fresh=False):
        visitor = blocks[first : first + count, rows_of_each, :]
        visitor = visitor.reshape(visitor.shape[0] * visitor.shape[1], visitor.shape[2])
        value = pull(blocks[own, cut(own_half), :], visitor, temper, offset)
        grads[target, cut(own_half), :] = value if fresh else grads[target, cut(own_half), :] + value

    def pass_on(chunk):
        arrived(T4, chunk, chunk + 1)
        send(T4, T5, chunk, partner)
        arrived(I2, chunk, chunk + 1)
        send(I2, I3, chunk, partner)

    def give(side, own_half):
        target = TEXT_BACK if side else IMAGE_ACROSS
        for chunk in range(own_half * half, (own_half + 1) * half):
            outbox[side, part(chunk), :] = grads[target, part(chunk), :].astype(outbox.dtype)
            copy = return_message(side, chunk)
            copy.start()
            started.append(copy)

    label_load.wait()
    anchor = lax.axis_index("wide") * narrow_count + narrow
    grads[IMAGE], grads[TEXT] = own_pairs(
        blocks[I0], blocks[T0], labels_row[...], anchor, temper, offset
    )
    whole(I0, I1).wait_recv()
    whole(T0, T1).wait_recv()
    add(IMAGE, I0, None, T1, count=1)
    add(TEXT, T0, None, I1, count=1)

    for chunk in range(half):
        pass_on(chunk)
    add(IMAGE_ACROSS, I2, 0, T0, fresh=True)
    add(TEXT_BACK, T4, 0, I0, fresh=True)
    arrived(T5, 0, half)
    add(IMAGE_ACROSS, I2, 0, T4, cut(0))
    arrived(I3, 0, half)
    add(TEXT_BACK, T4, 0, I2, cut(0))
    for chunk in range(half, CHUNKS):
        pass_on(chunk)
        arrived(T5, chunk, chunk + 1)
        add(IMAGE_ACROSS, I2, 0, T4, part(chunk))
        if chunk == CHUNKS - 1:
            give(IMAGE, 0)
        arrived(I3, chunk, chunk + 1)
        add(TEXT_BACK, T4, 0, I2, part(chunk))
    give(TEXT, 0)
    add(IMAGE_ACROSS, I2, 1, T0, count=4, fresh=True)
    give(IMAGE, 1)
    add(TEXT_BACK, T4, 1, I0, count=4, fresh=True)
    give(TEXT, 1)
    add(IMAGE, I0, None, T4)
    add(TEXT, T0, None, I2)

    for chunk in range(CHUNKS):
        for side, out in ((IMAGE, grad_images_ref), (TEXT, grad_texts_ref)):
            return_message(side, chunk).wait_recv()
            unit, inverse = normalize(raw[side, part(chunk), :])
            total = grads[side, part(chunk), :] + inbox[side, part(chunk), :].astype(jnp.float32)
            out[part(chunk), :] = unit_backward(unit, inverse, total)
    for copy in started:
        copy.wait_send()


def direct_kernel(
    wide_count,
    narrow_count,
    log_scale_ref,
    bias_ref,
    images_ref,
    texts_ref,
    labels_ref,
    grad_images_ref,
    grad_texts_ref,
    labels_row,
    blocks,
    grads,
    load_sem,
    send_sem,
    recv_sem,
):
    rows = blocks.shape[2]
    wide = lax.axis_index("wide")
    narrow = lax.axis_index("narrow")
    slots = 2 * WINDOW
    targets = {}
    for side, sign in ((IMAGE, -1), (TEXT, 1)):
        for slot in range(1, slots):
            wide_back = slot // WINDOW
            narrow_back = slot - wide_back * WINDOW + wide_back * (WINDOW - 1)
            index = lax.rem(narrow + sign * narrow_back + 2 * narrow_count, narrow_count)
            targets[side, slot] = place(wide_count, sign * wide_back, index)
    load = pltpu.make_async_copy(labels_ref, labels_row, load_sem.at[0])
    load.start()
    barrier = greet(targets.values())

    temper = jnp.exp(jnp.full((1, 1), log_scale_ref[0], jnp.float32))
    offset = bias_ref[0]
    sources = {IMAGE: images_ref, TEXT: texts_ref}
    for side in (IMAGE, TEXT):
        blocks[side, 0] = normalize(sources[side][...])[0].astype(jnp.bfloat16)
    pl.semaphore_wait(barrier, len(targets))
    copies = {}
    for slot in range(1, slots):
        for side in (IMAGE, TEXT):
            copies[side, slot] = pltpu.make_async_remote_copy(
                src_ref=blocks.at[side, 0],
                dst_ref=blocks.at[side, slot],
                send_sem=send_sem.at[side, slot],
                recv_sem=recv_sem.at[side, slot],
                device_id=targets[side, slot],
                device_id_type=MESH,
            )
            copies[side, slot].start()
    load.wait()
    grads[IMAGE], grads[TEXT] = own_pairs(
        blocks[IMAGE, 0], blocks[TEXT, 0], labels_row[...], wide * narrow_count + narrow, temper, offset
    )
    for copy in copies.values():
        copy.wait_recv()

    @pl.loop(2, 2 * slots)
    def _(step):
        side = lax.rem(step, 2)
        grads[1 - side] += pull(blocks[1 - side, 0], blocks[side, step // 2], temper, offset)

    for side, out in ((IMAGE, grad_images_ref), (TEXT, grad_texts_ref)):
        unit, inverse = normalize(sources[side][...])
        out[...] = unit_backward(unit, inverse, grads[side])
    for copy in copies.values():
        copy.wait_send()


def shards(images, texts, labels, log_scale, bias):
    rows, depth = images.shape
    wide_count = lax.axis_size("wide")
    narrow_count = lax.axis_size("narrow")
    vmem = pl.BlockSpec(memory_space=pltpu.VMEM)
    smem = pl.BlockSpec(memory_space=pltpu.SMEM)
    hbm = pl.BlockSpec(memory_space=pltpu.HBM)
    row = pltpu.VMEM((1, rows), jnp.int32)
    dma = pltpu.SemaphoreType.DMA
    out = jax.ShapeDtypeStruct((rows, depth), jnp.float32)
    pairs = 2 * 2 * WINDOW * rows * rows
    if narrow_count == WINDOW:
        body, held = relay_kernel, hbm
        scratch = [
            pltpu.VMEM((2, rows, depth), images.dtype),
            row,
            pltpu.VMEM((2 * WINDOW, rows, depth), jnp.bfloat16),
            pltpu.VMEM((4, rows, depth), jnp.float32),
            pltpu.VMEM((2, rows, depth), jnp.bfloat16),
            pltpu.VMEM((2, rows, depth), jnp.bfloat16),
            dma((3, CHUNKS)),
            dma((2 * WINDOW, CHUNKS)),
            dma((2 * WINDOW, CHUNKS)),
            dma((2, CHUNKS)),
            dma((2, CHUNKS)),
        ]
    else:
        body, held = direct_kernel, vmem
        scratch = [
            row,
            pltpu.VMEM((2, 2 * WINDOW, rows, depth), jnp.bfloat16),
            pltpu.VMEM((2, rows, depth), jnp.float32),
            dma((1,)),
            dma((2, 2 * WINDOW)),
            dma((2, 2 * WINDOW)),
        ]
    arrays = (images, texts, labels.reshape(1, rows))
    if held is hbm:
        arrays = tuple(pltpu.with_memory_space_constraint(array, pltpu.HBM) for array in arrays)
    return pl.pallas_call(
        functools.partial(body, wide_count, narrow_count),
        out_shape=(out, out),
        in_specs=[smem, smem, held, held, hbm],
        out_specs=(vmem, vmem),
        scratch_shapes=scratch,
        compiler_params=pltpu.CompilerParams(
            collective_id=0, has_side_effects=True, vmem_limit_bytes=40 * 1024 * 1024
        ),
        cost_estimate=pl.CostEstimate(
            flops=4 * pairs * depth, bytes_accessed=12 * rows * depth, transcendentals=pairs
        ),
        name="window_grads",
    )(log_scale, bias, *arrays)

def solution(mesh):
    return jax.shard_map(
        shards,
        mesh=mesh,
        in_specs=(
            P(("wide", "narrow"), None),
            P(("wide", "narrow"), None),
            P(("wide", "narrow")),
            P(),
            P(),
        ),
        out_specs=(P(("wide", "narrow"), None), P(("wide", "narrow"), None)),
        check_vma=False,
    )
```

```python
import functools

import jax
import jax.numpy as jnp
from jax import lax
from jax.experimental import pallas as pl
from jax.experimental.pallas import tpu as pltpu
from jax.sharding import PartitionSpec as P

WINDOW = 4
EPS = 1e-06
CHUNKS = 2
MESH = pl.DeviceIdType.MESH


def normalize(vectors):
    floats = vectors.astype(jnp.float32)
    inverse = lax.rsqrt(jnp.sum(floats * floats, axis=-1, keepdims=True) + EPS)
    return (floats * inverse, inverse)


def unit_backward(unit_rows, inverse, upstream):
    return inverse * (upstream - unit_rows * jnp.sum(unit_rows * upstream, axis=-1, keepdims=True))


def place(wide_count, wide_step, narrow_index):
    return (lax.rem(lax.axis_index("wide") + wide_step + wide_count, wide_count), narrow_index)


def greet(neighbours):
    barrier = pltpu.get_barrier_semaphore()
    for neighbour in neighbours:
        pl.semaphore_signal(barrier, inc=1, device_id=neighbour, device_id_type=MESH)
    return barrier


def probability(own, visitor, temper, offset):
    scores = lax.dot_general(
        own, visitor, (((1,), (1,)), ((), ())), preferred_element_type=jnp.float32
    )
    return jax.nn.sigmoid(temper * scores + offset)


def pull(own, visitor, temper, offset):
    weighted = (temper * probability(own, visitor, temper, offset)).astype(jnp.bfloat16)
    return jnp.dot(weighted, visitor, preferred_element_type=jnp.float32)


def own_pairs(image_rows, text_rows, labels_row, anchor, temper, offset):
    rows = image_rows.shape[0]
    target = anchor * rows + lax.broadcasted_iota(jnp.int32, (rows, rows), 0)
    positive = (labels_row == target).astype(jnp.float32)
    residual = probability(text_rows, image_rows, temper, offset) - positive
    weighted = (temper * residual).astype(jnp.bfloat16)
    image_grad = lax.dot_general(
        weighted, text_rows, (((0,), (0,)), ((), ())), preferred_element_type=jnp.float32
    )
    return image_grad, jnp.dot(weighted, image_rows, preferred_element_type=jnp.float32)


IMAGE, TEXT, IMAGE_ACROSS, TEXT_BACK = range(4)
I0, I1, I2, I3, T0, T1, T4, T5 = range(8)


def relay_kernel(
    wide_count,
    narrow_count,
    log_scale_ref,
    bias_ref,
    images_ref,
    texts_ref,
    labels_ref,
    grad_images_ref,
    grad_texts_ref,
    raw,
    labels_row,
    blocks,
    grads,
    outbox,
    inbox,
    load_sem,
    send_sem,
    recv_sem,
    grad_send_sem,
    grad_recv_sem,
):
    rows = blocks.shape[1]
    piece = rows // CHUNKS
    half = CHUNKS // 2
    narrow = lax.axis_index("narrow")
    partner = place(wide_count, 0, narrow + 1 - 2 * lax.rem(narrow, 2))
    across = place(wide_count, 0, lax.rem(narrow + 2, narrow_count))
    forth = place(wide_count, 1, narrow)
    back = place(wide_count, -1, narrow)
    neighbours = [partner, across, forth, back]

    def part(chunk):
        return pl.ds(chunk * piece, piece)

    sources = ((I0, raw.at[IMAGE], images_ref), (T0, raw.at[TEXT], texts_ref))
    loads = [
        [
            pltpu.make_async_copy(ref.at[part(chunk)], target.at[part(chunk)], load_sem.at[number, chunk])
            for number, (_, target, ref) in enumerate(sources)
        ]
        for chunk in range(CHUNKS)
    ]
    for pair in loads:
        for load in pair:
            load.start()
    label_load = pltpu.make_async_copy(labels_ref, labels_row, load_sem.at[2, 0])
    label_load.start()
    barrier = greet(neighbours)

    temper = jnp.exp(jnp.full((1, 1), log_scale_ref[0], jnp.float32))
    offset = bias_ref[0]
    started = []

    def message(source, slot, chunk, target):
        return pltpu.make_async_remote_copy(
            src_ref=blocks.at[source, part(chunk)],
            dst_ref=blocks.at[slot, part(chunk)],
            send_sem=send_sem.at[slot, chunk],
            recv_sem=recv_sem.at[slot, chunk],
            device_id=target,
            device_id_type=MESH,
        )

    def send(source, slot, chunk, target):
        copy = message(source, slot, chunk, target)
        copy.start()
        started.append(copy)

    def whole(source, slot):
        return pltpu.make_async_remote_copy(
            src_ref=blocks.at[source],
            dst_ref=blocks.at[slot],
            send_sem=send_sem.at[slot, 0],
            recv_sem=recv_sem.at[slot, 0],
            device_id=partner,
            device_id_type=MESH,
        )

    def arrived(slot, first, last):
        for chunk in range(first, last):
            message(slot, slot, chunk, partner).wait_recv()

    def return_message(side, chunk):
        return pltpu.make_async_remote_copy(
            src_ref=outbox.at[side, part(chunk)],
            dst_ref=inbox.at[side, part(chunk)],
            send_sem=grad_send_sem.at[side, chunk],
            recv_sem=grad_recv_sem.at[side, chunk],
            device_id=back if side else across,
            device_id_type=MESH,
        )

    for chunk in range(CHUNKS):
        for load in loads[chunk]:
            load.wait()
        for slot, source, _ in sources:
            unit, _ = normalize(source[part(chunk), :])
            blocks[slot, part(chunk), :] = unit.astype(jnp.bfloat16)
        if chunk == 0:
            pl.semaphore_wait(barrier, len(neighbours))
        send(I0, I2, chunk, across)
        send(T0, T4, chunk, forth)
    for slot, source in ((I1, I0), (T1, T0)):
        started.append(whole(source, slot))
        started[-1].start()

    def cut(half_or_all):
        return slice(None) if half_or_all is None else pl.ds(half_or_all * half * piece, half * piece)

    def add(target, own, own_half, first, rows_of_each=slice(None), count=2, fresh=False, leaving=None):
        visitor = blocks[first : first + count, rows_of_each, :]
        visitor = visitor.reshape(visitor.shape[0] * visitor.shape[1], visitor.shape[2])
        value = pull(blocks[own, cut(own_half), :], visitor, temper, offset)
        total = value if fresh else grads[target, cut(own_half), :] + value
        if leaving is None:
            grads[target, cut(own_half), :] = total
            return
        outbox[leaving, cut(own_half), :] = total.astype(outbox.dtype)
        for chunk in range(own_half * half, (own_half + 1) * half):
            copy = return_message(leaving, chunk)
            copy.start()
            started.append(copy)

    def pass_on(chunk):
        arrived(T4, chunk, chunk + 1)
        send(T4, T5, chunk, partner)
        arrived(I2, chunk, chunk + 1)
        send(I2, I3, chunk, partner)

    label_load.wait()
    anchor = lax.axis_index("wide") * narrow_count + narrow
    grads[IMAGE], grads[TEXT] = own_pairs(
        blocks[I0], blocks[T0], labels_row[...], anchor, temper, offset
    )
    whole(I0, I1).wait_recv()
    whole(T0, T1).wait_recv()
    add(IMAGE, I0, None, T1, count=1)
    add(TEXT, T0, None, I1, count=1)

    for chunk in range(half):
        pass_on(chunk)
    add(IMAGE_ACROSS, I2, 0, T0, fresh=True)
    add(TEXT_BACK, T4, 0, I0, fresh=True)
    arrived(T5, 0, half)
    add(IMAGE_ACROSS, I2, 0, T4, cut(0))
    arrived(I3, 0, half)
    add(TEXT_BACK, T4, 0, I2, cut(0))
    for chunk in range(half, CHUNKS):
        last = chunk == CHUNKS - 1
        pass_on(chunk)
        arrived(T5, chunk, chunk + 1)
        add(IMAGE_ACROSS, I2, 0, T4, part(chunk), leaving=IMAGE if last else None)
        arrived(I3, chunk, chunk + 1)
        add(TEXT_BACK, T4, 0, I2, part(chunk), leaving=TEXT if last else None)
    add(IMAGE_ACROSS, I2, 1, T0, count=4, fresh=True, leaving=IMAGE)
    add(TEXT_BACK, T4, 1, I0, count=4, fresh=True, leaving=TEXT)
    add(IMAGE, I0, None, T4)
    add(TEXT, T0, None, I2)

    for chunk in range(CHUNKS):
        for side, out in ((IMAGE, grad_images_ref), (TEXT, grad_texts_ref)):
            return_message(side, chunk).wait_recv()
            unit, inverse = normalize(raw[side, part(chunk), :])
            total = grads[side, part(chunk), :] + inbox[side, part(chunk), :].astype(jnp.float32)
            out[part(chunk), :] = unit_backward(unit, inverse, total)
    for copy in started:
        copy.wait_send()


def direct_kernel(
    wide_count,
    narrow_count,
    log_scale_ref,
    bias_ref,
    images_ref,
    texts_ref,
    labels_ref,
    grad_images_ref,
    grad_texts_ref,
    labels_row,
    blocks,
    grads,
    load_sem,
    send_sem,
    recv_sem,
):
    rows = blocks.shape[2]
    wide = lax.axis_index("wide")
    narrow = lax.axis_index("narrow")
    slots = 2 * WINDOW
    targets = {}
    for side, sign in ((IMAGE, -1), (TEXT, 1)):
        for slot in range(1, slots):
            wide_back = slot // WINDOW
            narrow_back = slot - wide_back * WINDOW + wide_back * (WINDOW - 1)
            index = lax.rem(narrow + sign * narrow_back + 2 * narrow_count, narrow_count)
            targets[side, slot] = place(wide_count, sign * wide_back, index)
    load = pltpu.make_async_copy(labels_ref, labels_row, load_sem.at[0])
    load.start()
    barrier = greet(targets.values())

    temper = jnp.exp(jnp.full((1, 1), log_scale_ref[0], jnp.float32))
    offset = bias_ref[0]
    sources = {IMAGE: images_ref, TEXT: texts_ref}
    for side in (IMAGE, TEXT):
        blocks[side, 0] = normalize(sources[side][...])[0].astype(jnp.bfloat16)
    pl.semaphore_wait(barrier, len(targets))
    copies = {}
    for slot in range(1, slots):
        for side in (IMAGE, TEXT):
            copies[side, slot] = pltpu.make_async_remote_copy(
                src_ref=blocks.at[side, 0],
                dst_ref=blocks.at[side, slot],
                send_sem=send_sem.at[side, slot],
                recv_sem=recv_sem.at[side, slot],
                device_id=targets[side, slot],
                device_id_type=MESH,
            )
            copies[side, slot].start()
    load.wait()
    grads[IMAGE], grads[TEXT] = own_pairs(
        blocks[IMAGE, 0], blocks[TEXT, 0], labels_row[...], wide * narrow_count + narrow, temper, offset
    )
    for copy in copies.values():
        copy.wait_recv()

    @pl.loop(2, 2 * slots)
    def _(step):
        side = lax.rem(step, 2)
        grads[1 - side] += pull(blocks[1 - side, 0], blocks[side, step // 2], temper, offset)

    for side, out in ((IMAGE, grad_images_ref), (TEXT, grad_texts_ref)):
        unit, inverse = normalize(sources[side][...])
        out[...] = unit_backward(unit, inverse, grads[side])
    for copy in copies.values():
        copy.wait_send()


def shards(images, texts, labels, log_scale, bias):
    rows, depth = images.shape
    wide_count = lax.axis_size("wide")
    narrow_count = lax.axis_size("narrow")
    vmem = pl.BlockSpec(memory_space=pltpu.VMEM)
    smem = pl.BlockSpec(memory_space=pltpu.SMEM)
    hbm = pl.BlockSpec(memory_space=pltpu.HBM)
    row = pltpu.VMEM((1, rows), jnp.int32)
    dma = pltpu.SemaphoreType.DMA
    out = jax.ShapeDtypeStruct((rows, depth), jnp.float32)
    pairs = 2 * 2 * WINDOW * rows * rows
    if narrow_count == WINDOW:
        body, held = relay_kernel, hbm
        scratch = [
            pltpu.VMEM((2, rows, depth), images.dtype),
            row,
            pltpu.VMEM((2 * WINDOW, rows, depth), jnp.bfloat16),
            pltpu.VMEM((4, rows, depth), jnp.float32),
            pltpu.VMEM((2, rows, depth), jnp.bfloat16),
            pltpu.VMEM((2, rows, depth), jnp.bfloat16),
            dma((3, CHUNKS)),
            dma((2 * WINDOW, CHUNKS)),
            dma((2 * WINDOW, CHUNKS)),
            dma((2, CHUNKS)),
            dma((2, CHUNKS)),
        ]
    else:
        body, held = direct_kernel, vmem
        scratch = [
            row,
            pltpu.VMEM((2, 2 * WINDOW, rows, depth), jnp.bfloat16),
            pltpu.VMEM((2, rows, depth), jnp.float32),
            dma((1,)),
            dma((2, 2 * WINDOW)),
            dma((2, 2 * WINDOW)),
        ]
    arrays = (images, texts, labels.reshape(1, rows))
    if held is hbm:
        arrays = tuple(pltpu.with_memory_space_constraint(array, pltpu.HBM) for array in arrays)
    return pl.pallas_call(
        functools.partial(body, wide_count, narrow_count),
        out_shape=(out, out),
        in_specs=[smem, smem, held, held, hbm],
        out_specs=(vmem, vmem),
        scratch_shapes=scratch,
        compiler_params=pltpu.CompilerParams(
            collective_id=0, has_side_effects=True, vmem_limit_bytes=40 * 1024 * 1024
        ),
        cost_estimate=pl.CostEstimate(
            flops=4 * pairs * depth, bytes_accessed=12 * rows * depth, transcendentals=pairs
        ),
        name="window_grads",
    )(log_scale, bias, *arrays)

def solution(mesh):
    return jax.shard_map(
        shards,
        mesh=mesh,
        in_specs=(
            P(("wide", "narrow"), None),
            P(("wide", "narrow"), None),
            P(("wide", "narrow")),
            P(),
            P(),
        ),
        out_specs=(P(("wide", "narrow"), None), P(("wide", "narrow"), None)),
        check_vma=False,
    )
```
